32 devices in a mesh: table: 8 (over y, x, core), batch: 4 (over z).
Axes of the slice: x: 2, y: 2, z: 4, core: 2. Of those that a mesh axis runs over, the one named last changes fastest.
Arguments:
- table_rows: float32 [192, 64, 128], P('table'), may hold values from -6 to 6
- accum: float32 [192, 64], P('table'), may hold values from 0.05 to 2
- plan_dest: int32 [8, 2], replicated, may hold values from 0 to 7, as said below
- plan_slot: int32 [8, 2], replicated, may hold values from 0 to 23, as said below
- bag_block: int32 [4096], P(('table', 'batch')), may hold values from 0 to 191, as said below
- bag_rows: int32 [4096, 8], P(('table', 'batch')), may hold values from 0 to 63
- grad_pooled: float32 [4096, 128], P(('table', 'batch')), may hold values from -6 to 6
Outputs:
- pooled: float32 [4096, 128], P(('table', 'batch'))
- table_new: float32 [192, 64, 128], P('table')
- accum_new: float32 [192, 64], P('table')
The draws below stay inside these ranges and needn't reach their ends.
Inputs may be any that keep to these rules, and one draw needn't show every extreme that they name: `plan_dest`: row s names 2 distinct owners, none equal to s; every owner is named in exactly 2 rows. `plan_slot`: the slots of one row are distinct. `bag_block`: after migration, at most 64 samples of one device read blocks held by one owner; in every draw some owner is read by exactly 64 samples of every device.
All inputs are finite; a program needn't handle non-finite values.
Results may differ from the reference program's by a relative error of at most 0.00002.
Values sent between devices are 32-bit elements; how exact they have to be, the bound alone decides.
A program may use at most 64 MiB of HBM per device.

```python
import math
import jax
import jax.numpy as jnp
from jax import lax

DIM = 128
BROWS = 64
BLK_DEV = 24
SAMP = 128
POOL = 8
MIG = 2
CAPS = 64
BLOCKS = 192
ALLS = 4096
N_TABLE = 8


def directory_drawn(plan_dest, plan_slot, blocks_each):
    n_owner, moving = plan_dest.shape
    sources = jnp.repeat(jnp.arange(n_owner, dtype=jnp.int32), moving)
    targets = plan_dest.reshape(-1).astype(jnp.int32)
    leaving = plan_slot.reshape(-1).astype(jnp.int32)
    earlier = (targets[:, None] == targets[None, :]) & (sources[None, :] < sources[:, None])
    arrival = jnp.sum(earlier.astype(jnp.int32), axis=1).astype(jnp.int32)
    landing = plan_slot[targets, arrival].astype(jnp.int32)
    old_spot = sources * blocks_each + leaving
    owner_of = jnp.repeat(jnp.arange(n_owner, dtype=jnp.int32), blocks_each).at[old_spot].set(targets)
    place_of = jnp.tile(jnp.arange(blocks_each, dtype=jnp.int32), n_owner).at[old_spot].set(landing)
    return (owner_of, place_of)


def plan_parts(key):
    key_order, key_offsets, key_slots = jax.random.split(key, 3)
    device_order = jax.random.permutation(key_order, N_TABLE).astype(jnp.int32)
    position = jnp.zeros((N_TABLE,), jnp.int32).at[device_order].set(jnp.arange(N_TABLE, dtype=jnp.int32))
    offsets = jax.random.permutation(key_offsets, N_TABLE - 1)[:MIG].astype(jnp.int32) + 1
    destinations = device_order[(position[:, None] + offsets[None, :]) % N_TABLE]
    slot_keys = jax.random.split(key_slots, N_TABLE)
    leaving = jax.vmap(lambda one_key: jax.random.permutation(one_key, BLK_DEV)[:MIG])(slot_keys)
    return (destinations.astype(jnp.int32), leaving.astype(jnp.int32))


def draw_plan_dest(key, part):
    destinations, leaving = plan_parts(key)
    return destinations


def draw_plan_slot(key, part):
    destinations, leaving = plan_parts(key)
    return leaving


def draw_bag_block(key, part):
    destinations, leaving = plan_parts(key)
    key = jax.random.fold_in(key, 7)
    owner_of, place_of = directory_drawn(destinations, leaving, BLK_DEV)
    new_index = owner_of * BLK_DEV + place_of
    inverse = jnp.zeros((N_TABLE * BLK_DEV,), jnp.int32).at[new_index].set(jnp.arange(N_TABLE * BLK_DEV, dtype=jnp.int32))
    key_hot, key_devices = jax.random.split(key)
    hot_owner = jax.random.randint(key_hot, (), 0, N_TABLE).astype(jnp.int32)

    def one_device(one_key):
        key_pick, key_shuffle, key_slot = jax.random.split(one_key, 3)
        other_owners = jnp.arange((N_TABLE - 1) * CAPS, dtype=jnp.int32) // CAPS
        other_owners = other_owners + (other_owners >= hot_owner).astype(jnp.int32)
        picked = jax.random.permutation(key_pick, other_owners)[:SAMP - CAPS]
        owner_list = jnp.concatenate([jnp.full((CAPS,), hot_owner, jnp.int32), picked])
        owner_list = jax.random.permutation(key_shuffle, owner_list)
        slot_list = jax.random.randint(key_slot, (SAMP,), 0, BLK_DEV).astype(jnp.int32)
        return inverse[owner_list * BLK_DEV + slot_list]
    device_keys = jax.random.split(key_devices, ALLS // SAMP)
    return jax.vmap(one_device)(device_keys).reshape(-1).astype(jnp.int32)


def plant(drawn, rng, smallest, high):
    spot = [jax.random.randint(jax.random.fold_in(rng, axis), (), 0, length) for axis, length in enumerate(drawn.shape)]
    longest = drawn.shape.index(max(drawn.shape))
    beside = spot[:longest] + [(spot[longest] + 1) % drawn.shape[longest]] + spot[longest + 1:]
    return drawn.at[tuple(spot)].set(smallest).at[tuple(beside)].set(high)


def level_of(rng, extent, cuts, low, top_value):
    factor_of = 1.0
    for dim, parts in cuts:
        steps = jax.random.uniform(jax.random.fold_in(jax.random.fold_in(rng, 6), dim), (parts,), jnp.float32, low / len(cuts), top_value / len(cuts))
        factor_of = factor_of * jnp.repeat(jnp.exp(steps), extent[dim] // parts).reshape((-1,) + (1,) * (len(extent) - 1 - dim))
    return factor_of


def gaussian(rng, dims, scale, limit, pieces=(), kind=jnp.bfloat16):
    entries = jax.random.normal(rng, dims, jnp.float32) * scale
    if len(pieces) > 0:
        entries = level_of(rng, dims, pieces, -0.22, 0.18) * entries
    return jnp.clip(entries, min=-limit, max=limit).astype(kind)


def setup_inputs(seed: int = 0) -> dict:
    arg_keys = jax.random.split(jax.random.key(seed), 8)
    table_rows = gaussian(arg_keys[0], (BLOCKS, BROWS, DIM), 1.0, 6.0, ((0, 8),), jnp.float32)
    accum = jnp.clip(jnp.exp(math.log(2.0) - 3.6888794 * jax.random.uniform(arg_keys[1], (BLOCKS, BROWS), jnp.float32) ** level_of(arg_keys[1], (BLOCKS, BROWS), ((0, 8),), -0.2, 0.2)), 0.05, 2.0)
    plan_dest = draw_plan_dest(jax.random.fold_in(arg_keys[7], 71), 0)
    plan_slot = draw_plan_slot(jax.random.fold_in(arg_keys[7], 71), 0)
    bag_block = draw_bag_block(jax.random.fold_in(arg_keys[7], 71), 0)
    bag_rows = plant(jax.random.randint(arg_keys[5], (ALLS, POOL), 0, BROWS), jax.random.fold_in(arg_keys[5], 1), 0, BROWS - 1).astype(jnp.int32)
    grad_pooled = gaussian(arg_keys[6], (ALLS, DIM), 1.0, 6.0, ((0, 32),), jnp.float32)
    return dict(table_rows=table_rows, accum=accum, plan_dest=plan_dest, plan_slot=plan_slot, bag_block=bag_block, bag_rows=bag_rows, grad_pooled=grad_pooled)


LEARN_RATE = 0.3
EPSILON = 1e-08

def directory(plan_dest, plan_slot, blocks_each):
    n_owner, moving = plan_dest.shape
    sources = jnp.repeat(jnp.arange(n_owner, dtype=jnp.int32), moving)
    targets = plan_dest.reshape(-1).astype(jnp.int32)
    leaving = plan_slot.reshape(-1).astype(jnp.int32)
    earlier = (targets[:, None] == targets[None, :]) & (sources[None, :] < sources[:, None])
    arrival = lax.optimization_barrier(jnp.sum(earlier.astype(jnp.int32), axis=1)).astype(jnp.int32)
    landing = plan_slot[targets, arrival].astype(jnp.int32)
    old_spot = sources * blocks_each + leaving
    new_spot = targets * blocks_each + landing
    owner_of = jnp.repeat(jnp.arange(n_owner, dtype=jnp.int32), blocks_each).at[old_spot].set(targets)
    place_of = jnp.tile(jnp.arange(blocks_each, dtype=jnp.int32), n_owner).at[old_spot].set(landing)
    return (owner_of, place_of, old_spot, new_spot)

def reference(table_rows, accum, plan_dest, plan_slot, bag_block, bag_rows, grad_pooled):
    owner_of, place_of, old_spot, new_spot = directory(plan_dest, plan_slot, BLK_DEV)
    moved = table_rows.at[new_spot].set(table_rows[old_spot])
    moved_acc = accum.at[new_spot].set(accum[old_spot])
    read_block = owner_of[bag_block] * BLK_DEV + place_of[bag_block]
    row_index = (read_block[:, None] * BROWS + bag_rows).astype(jnp.int32)
    flat_rows = moved.reshape(-1, DIM)
    pooled = lax.optimization_barrier(jnp.sum(flat_rows[row_index], axis=1))
    spread = jnp.broadcast_to(grad_pooled[:, None, :], row_index.shape + (DIM,)).reshape(-1, DIM)
    row_grad = jax.ops.segment_sum(spread, row_index.reshape(-1), num_segments=flat_rows.shape[0])
    acc_new = moved_acc.reshape(-1) + lax.optimization_barrier(jnp.mean(row_grad * row_grad, axis=1))
    table_new = flat_rows - LEARN_RATE * row_grad / (jnp.sqrt(acc_new)[:, None] + EPSILON)
    return (pooled, table_new.reshape(moved.shape), acc_new.reshape(moved_acc.shape))
```

```python
import functools

import jax
import jax.numpy as jnp
from jax import lax
from jax.experimental import pallas as pl
from jax.experimental.pallas import tpu as pltpu
from jax.sharding import PartitionSpec as P

LEARN_RATE = 0.3
EPSILON = 1e-08
MESH = pl.DeviceIdType.MESH
EXACT = lax.Precision.HIGHEST


def split_halves(values):
    high = values.astype(jnp.bfloat16)
    low = (values - high.astype(jnp.float32)).astype(jnp.bfloat16)
    return jnp.concatenate([high, low], axis=1)


def kernel(
    n, reps, cap,
    picked, source, bucket_row, bucket_col, lane_col, rows_t, table, accum, grad,
    pooled_out, table_out, accum_out,
    comb, mig_send, ids_send, grad_send, grads, ids, moved_hl, total, pool_part, pool_back,
    send_sem, recv_sem, zsend_sem, zrecv_sem, psend_sem, precv_sem,
):
    me = lax.axis_index("table")
    rep = lax.axis_index("batch")
    blocks, brows, dim = table.shape
    samples = grad.shape[0]
    slots = n * cap
    groups = slots // 128
    per_group = 128 // cap
    has_up = rep < reps - 1
    has_down = rep > 0
    step_blocks = 4 if blocks % 4 == 0 else 1

    barrier = pltpu.get_barrier_semaphore()
    for d in range(1, n):
        pl.semaphore_signal(
            barrier, inc=1, device_id={"table": lax.rem(me + d, n)}, device_id_type=MESH
        )

    @pl.when(has_up)
    def _():
        pl.semaphore_signal(barrier, inc=1, device_id={"batch": rep + 1}, device_id_type=MESH)

    @pl.when(has_down)
    def _():
        pl.semaphore_signal(barrier, inc=1, device_id={"batch": rep - 1}, device_id_type=MESH)

    place = (
        lax.broadcasted_iota(jnp.int32, (slots, samples), 0) == bucket_row[...]
    ).astype(jnp.float32)
    sent = jnp.dot(place, grad[...], precision=EXACT, preferred_element_type=jnp.float32)
    grad_send[...] = sent.reshape(n, cap, dim)
    lanes = (
        lax.broadcasted_iota(jnp.int32, (samples, n * 128), 1) == lane_col[...]
    ).astype(jnp.float32)
    sent_ids = jnp.dot(rows_t[...], lanes, precision=EXACT, preferred_element_type=jnp.float32)
    for d in range(n):
        ids_send[d] = sent_ids[:, d * 128 : (d + 1) * 128]

    for d in range(n):
        mig_send[d, 0:brows, :] = table[picked[d]]
        mig_send[d, brows:, :] = jnp.zeros((8, dim), jnp.float32)
        mig_send[d, brows : brows + 1, 0:brows] = accum[pl.ds(picked[d], 1), :]

    neighbours = jnp.where(has_up, 1, 0) + jnp.where(has_down, 1, 0)
    pl.semaphore_wait(barrier, n - 1 + neighbours)

    def exchange(kind, src, dst, peer):
        return pltpu.make_async_remote_copy(
            src_ref=src, dst_ref=dst,
            send_sem=send_sem.at[kind, peer], recv_sem=recv_sem.at[kind, me],
            device_id={"table": peer}, device_id_type=MESH,
        )

    def arrival(kind, dst, peer):
        return pltpu.make_async_remote_copy(
            src_ref=dst, dst_ref=dst,
            send_sem=send_sem.at[kind, peer], recv_sem=recv_sem.at[kind, peer],
            device_id={"table": peer}, device_id_type=MESH,
        )

    peers = [lax.rem(me + d, n) for d in range(1, n)]
    for peer in peers:
        exchange(0, ids_send.at[peer], ids.at[rep, me], peer).start()
        exchange(1, grad_send.at[peer], grads.at[rep, me], peer).start()
    for peer in peers:
        exchange(2, mig_send.at[peer], comb.at[blocks + me], peer).start()
    ids[rep, me] = ids_send[me]
    grads[rep, me] = grad_send[me]

    comb[0:blocks, 0:brows, :] = table[...]
    comb[0:blocks, brows:, :] = jnp.zeros((blocks, 8, dim), jnp.float32)
    comb[blocks + me] = jnp.zeros((brows + 8, dim), jnp.float32)
    for j in range(blocks):
        comb[j, brows : brows + 1, 0:brows] = accum[j : j + 1, :]

    for peer in peers:
        arrival(0, ids.at[rep, peer], peer).wait_recv()
        arrival(1, grads.at[rep, peer], peer).wait_recv()

    def hop(kind, way, origin):
        buffer = ids if kind == 0 else grads
        return pltpu.make_async_remote_copy(
            src_ref=buffer.at[origin], dst_ref=buffer.at[origin],
            send_sem=zsend_sem.at[way, kind, origin], recv_sem=zrecv_sem.at[kind, origin],
            device_id={"batch": rep + 1 - 2 * way}, device_id_type=MESH,
        )

    def send_on(way, origin):
        for kind in range(2):
            hop(kind, way, origin).start()

    @pl.when(has_up)
    def _():
        send_on(0, rep)

    @pl.when(has_down)
    def _():
        send_on(1, rep)

    for peer in peers:
        arrival(2, comb.at[blocks + peer], peer).wait_recv()

    row_id = lax.broadcasted_iota(jnp.int32, (brows, 128), 0)

    def counts_of(origin):
        places, counts = [], []
        for g in range(groups):
            named = ids[origin, g * per_group]
            for s in range(1, per_group):
                named = named + ids[origin, g * per_group + s]
            named = named.astype(jnp.int32) - 1
            places.append(jnp.right_shift(named[0:1, :], (brows - 1).bit_length()))
            rows = jnp.bitwise_and(named, brows - 1)
            count = jnp.zeros((brows, 128), jnp.float32)
            for k in range(rows.shape[0]):
                count = count + (rows[k : k + 1, :] == row_id).astype(jnp.float32)
            counts.append(count)
        return jnp.concatenate(places, axis=1), jnp.concatenate(counts, axis=1)

    def chosen(places, counts, first):
        return jnp.concatenate(
            [
                jnp.where(places == first + b, counts, 0.0).astype(jnp.bfloat16)
                for b in range(step_blocks)
            ],
            axis=0,
        )

    span = step_blocks * brows

    def copy_moved(j, carry):
        moved_hl[pl.ds(pl.multiple_of(j * brows, brows), brows), :] = split_halves(
            comb[source[j], 0:brows, :]
        )
        return carry

    lax.fori_loop(0, blocks, copy_moved, 0)

    pool_part[...] = jnp.zeros_like(pool_part)
    places, counts = counts_of(rep)
    gradients = split_halves(grads[rep].reshape(slots, dim))

    def own_step(i, carry):
        hits = chosen(places, counts, i * step_blocks)
        where = pl.ds(pl.multiple_of(i * span, span), span)
        total[where, :] = jnp.dot(hits, gradients, preferred_element_type=jnp.float32)
        both = lax.dot_general(
            hits, moved_hl[where, :], (((0,), (0,)), ((), ())),
            preferred_element_type=jnp.float32,
        )
        pool_part[...] += (both[:, :dim] + both[:, dim:]).reshape(n, cap, dim)
        return carry

    lax.fori_loop(0, blocks // step_blocks, own_step, 0)

    def give_back(peer):
        return pltpu.make_async_remote_copy(
            src_ref=pool_part.at[peer], dst_ref=pool_back.at[me],
            send_sem=psend_sem.at[peer], recv_sem=precv_sem.at[me],
            device_id={"table": peer}, device_id_type=MESH,
        )

    def given_back(peer):
        return pltpu.make_async_remote_copy(
            src_ref=pool_part.at[peer], dst_ref=pool_back.at[peer],
            send_sem=psend_sem.at[peer], recv_sem=precv_sem.at[peer],
            device_id={"table": peer}, device_id_type=MESH,
        )

    for peer in peers:
        give_back(peer).start()
    pool_back[me] = pool_part[me]

    def add_origin(origin):
        places, counts = counts_of(origin)
        gradients = split_halves(grads[origin].reshape(slots, dim))

        def step(i, carry):
            hits = chosen(places, counts, i * step_blocks)
            where = pl.ds(pl.multiple_of(i * span, span), span)
            total[where, :] += jnp.dot(hits, gradients, preferred_element_type=jnp.float32)
            return carry

        lax.fori_loop(0, blocks // step_blocks, step, 0)

    def far_step(h, carry):
        below = rep - h
        above = rep + h

        @pl.when(below >= 0)
        def _():
            for kind in range(2):
                hop(kind, 0, below).wait_recv()

            @pl.when(has_up)
            def _():
                send_on(0, below)

        @pl.when(above < reps)
        def _():
            for kind in range(2):
                hop(kind, 1, above).wait_recv()

            @pl.when(has_down)
            def _():
                send_on(1, above)

        @pl.when(below >= 0)
        def _():
            add_origin(below)

        @pl.when(above < reps)
        def _():
            add_origin(above)

        return carry

    lax.fori_loop(1, reps, far_step, 0)

    eye = lax.broadcasted_iota(jnp.int32, (brows, brows), 0) == lax.broadcasted_iota(
        jnp.int32, (brows, brows), 1
    )

    def update(j, carry):
        where = pl.ds(pl.multiple_of(j * brows, brows), brows)
        both = total[where, :]
        row_grad = both[:, :dim] + both[:, dim:]
        at = source[j]
        old = comb[at, brows : brows + 1, 0:brows]
        old = jnp.sum(jnp.where(eye, old, 0.0), axis=1, keepdims=True)
        new = old + jnp.mean(row_grad * row_grad, axis=1, keepdims=True)
        table_out[j] = comb[at, 0:brows, :] - (LEARN_RATE * row_grad) / (jnp.sqrt(new) + EPSILON)
        accum_out[pl.ds(j, 1), :] = jnp.sum(jnp.where(eye, new, 0.0), axis=0, keepdims=True)
        return carry

    lax.fori_loop(0, blocks, update, 0)

    for peer in peers:
        given_back(peer).wait_recv()
    back = (
        lax.broadcasted_iota(jnp.int32, (samples, slots), 1) == bucket_col[...]
    ).astype(jnp.float32)
    pooled_out[...] = jnp.dot(
        back, pool_back[...].reshape(slots, dim), precision=EXACT,
        preferred_element_type=jnp.float32,
    )

    for peer in peers:
        exchange(0, ids_send.at[peer], ids.at[rep, me], peer).wait_send()
        exchange(1, grad_send.at[peer], grads.at[rep, me], peer).wait_send()
        exchange(2, mig_send.at[peer], comb.at[blocks + me], peer).wait_send()
        give_back(peer).wait_send()

    def drain(origin, carry):
        @pl.when(jnp.logical_and(has_up, origin <= rep))
        def _():
            for kind in range(2):
                hop(kind, 0, origin).wait_send()

        @pl.when(jnp.logical_and(has_down, origin >= rep))
        def _():
            for kind in range(2):
                hop(kind, 1, origin).wait_send()

        return carry

    lax.fori_loop(0, reps, drain, 0)


def per_device(table_rows, accum, plan_dest, plan_slot, bag_block, bag_rows, grad_pooled):
    blocks, brows, dim = table_rows.shape
    n = lax.axis_size("table")
    reps = lax.axis_size("batch")
    me = lax.axis_index("table")
    moving = plan_dest.shape[1]
    samples, pool = bag_rows.shape
    cap = 4 * samples // n
    owners = jnp.arange(n, dtype=jnp.int32)

    targets = plan_dest.reshape(-1)
    sources = jnp.arange(n * moving, dtype=jnp.int32) // moving
    earlier = (targets[:, None] == targets[None, :]) & (sources[None, :] < sources[:, None])
    rank = jnp.sum(earlier.astype(jnp.int32), axis=1)
    landing_at = targets * moving + rank
    every = jnp.arange(n * moving, dtype=jnp.int32)
    landing = jnp.sum(
        jnp.where(landing_at[:, None] == every[None, :], plan_slot.reshape(-1)[None, :], 0), axis=1
    )
    old_spot = sources * blocks + plan_slot.reshape(-1)
    new_spot = targets * blocks + landing

    mine = sources == me
    picked = jnp.sum(
        jnp.where(
            mine[None, :] & (targets[None, :] == owners[:, None]), plan_slot.reshape(-1)[None, :], 0
        ),
        axis=1,
    )
    spots = me * blocks + jnp.arange(blocks, dtype=jnp.int32)
    comes = new_spot[None, :] == spots[:, None]
    source = jnp.where(
        jnp.any(comes, axis=1),
        blocks + jnp.sum(jnp.where(comes, sources[None, :], 0), axis=1),
        jnp.arange(blocks, dtype=jnp.int32),
    )

    moves = bag_block[:, None] == old_spot[None, :]
    read = bag_block + jnp.sum(jnp.where(moves, (new_spot - old_spot)[None, :], 0), axis=1)
    owner = read // blocks
    order = jnp.arange(samples, dtype=jnp.int32)
    slot = jnp.sum(
        ((owner[:, None] == owner[None, :]) & (order[None, :] < order[:, None])).astype(jnp.int32),
        axis=1,
    )
    bucket = owner * cap + slot
    lane = owner * 128 + (me % (128 // cap)) * cap + slot
    rows_t = (((read - owner * blocks) * brows)[None, :] + bag_rows.T + 1).astype(jnp.float32)

    vmem = pl.BlockSpec(memory_space=pltpu.VMEM)
    smem = pl.BlockSpec(memory_space=pltpu.SMEM)
    slots = n * cap
    f32 = jnp.float32
    return pl.pallas_call(
        functools.partial(kernel, n, reps, cap),
        out_shape=(
            jax.ShapeDtypeStruct((samples, dim), f32),
            jax.ShapeDtypeStruct((blocks, brows, dim), f32),
            jax.ShapeDtypeStruct((blocks, brows), f32),
        ),
        in_specs=[smem] * 2 + [vmem] * 7,
        out_specs=(vmem, vmem, vmem),
        scratch_shapes=[
            pltpu.VMEM((blocks + n, brows + 8, dim), f32),
            pltpu.VMEM((n, brows + 8, dim), f32),
            pltpu.VMEM((n, pool, 128), f32),
            pltpu.VMEM((n, cap, dim), f32),
            pltpu.VMEM((reps, n, cap, dim), f32),
            pltpu.VMEM((reps, n, pool, 128), f32),
            pltpu.VMEM((blocks * brows, 2 * dim), jnp.bfloat16),
            pltpu.VMEM((blocks * brows, 2 * dim), f32),
            pltpu.VMEM((n, cap, dim), f32),
            pltpu.VMEM((n, cap, dim), f32),
            pltpu.SemaphoreType.DMA((3, n)),
            pltpu.SemaphoreType.DMA((3, n)),
            pltpu.SemaphoreType.DMA((2, 2, reps)),
            pltpu.SemaphoreType.DMA((2, reps)),
            pltpu.SemaphoreType.DMA((n,)),
            pltpu.SemaphoreType.DMA((n,)),
        ],
        compiler_params=pltpu.CompilerParams(
            collective_id=0, has_side_effects=True, vmem_limit_bytes=48 * 1024 * 1024
        ),
    )(
        picked, source, bucket[None, :], bucket[:, None], lane[:, None], rows_t,
        table_rows, accum, grad_pooled,
    )


def solution(mesh):
    return jax.shard_map(
        per_device,
        mesh=mesh,
        in_specs=(
            P("table", None, None),
            P("table", None),
            P(),
            P(),
            P(("table", "batch")),
            P(("table", "batch"), None),
            P(("table", "batch"), None),
        ),
        out_specs=(P(("table", "batch"), None), P("table", None, None), P("table", None)),
        check_vma=False,
    )
```

```python
import functools

import jax
import jax.numpy as jnp
from jax import lax
from jax.experimental import pallas as pl
from jax.experimental.pallas import tpu as pltpu
from jax.sharding import PartitionSpec as P

LEARN_RATE = 0.3
EPSILON = 1e-08
MESH = pl.DeviceIdType.MESH
EXACT = lax.Precision.HIGHEST


def split_halves(values):
    high = values.astype(jnp.bfloat16)
    low = (values - high.astype(jnp.float32)).astype(jnp.bfloat16)
    return jnp.concatenate([high, low], axis=1)


def bucket_kernel(
    n, reps, cap,
    picked, source, bucket_row, bucket_col, lane_col, rows_t, table, accum, grad,
    pooled_out, table_out, accum_out,
    comb, mig_send, ids_send, grad_send, grads, ids, moved_hl, total, pool_part, pool_back,
    send_sem, recv_sem, zsend_sem, zrecv_sem, psend_sem, precv_sem,
):
    me = lax.axis_index("table")
    rep = lax.axis_index("batch")
    blocks, brows, dim = table.shape
    samples = grad.shape[0]
    slots = n * cap
    groups = slots // 128
    per_group = 128 // cap
    has_up = rep < reps - 1
    has_down = rep > 0
    step_blocks = 4 if blocks % 4 == 0 else 1

    barrier = pltpu.get_barrier_semaphore()
    for d in range(1, n):
        pl.semaphore_signal(
            barrier, inc=1, device_id={"table": lax.rem(me + d, n)}, device_id_type=MESH
        )

    @pl.when(has_up)
    def _():
        pl.semaphore_signal(barrier, inc=1, device_id={"batch": rep + 1}, device_id_type=MESH)

    @pl.when(has_down)
    def _():
        pl.semaphore_signal(barrier, inc=1, device_id={"batch": rep - 1}, device_id_type=MESH)

    place = (
        lax.broadcasted_iota(jnp.int32, (slots, samples), 0) == bucket_row[...]
    ).astype(jnp.float32)
    sent = jnp.dot(place, grad[...], precision=EXACT, preferred_element_type=jnp.float32)
    grad_send[...] = sent.reshape(n, cap, dim)
    lanes = (
        lax.broadcasted_iota(jnp.int32, (samples, n * 128), 1) == lane_col[...]
    ).astype(jnp.float32)
    sent_ids = jnp.dot(rows_t[...], lanes, precision=EXACT, preferred_element_type=jnp.float32)
    for d in range(n):
        ids_send[d] = sent_ids[:, d * 128 : (d + 1) * 128]

    for d in range(n):
        mig_send[d, 0:brows, :] = table[picked[d]]
        mig_send[d, brows:, :] = jnp.zeros((8, dim), jnp.float32)
        mig_send[d, brows : brows + 1, 0:brows] = accum[pl.ds(picked[d], 1), :]

    neighbours = jnp.where(has_up, 1, 0) + jnp.where(has_down, 1, 0)
    pl.semaphore_wait(barrier, n - 1 + neighbours)

    def exchange(kind, src, dst, peer):
        return pltpu.make_async_remote_copy(
            src_ref=src, dst_ref=dst,
            send_sem=send_sem.at[kind, peer], recv_sem=recv_sem.at[kind, me],
            device_id={"table": peer}, device_id_type=MESH,
        )

    def arrival(kind, dst, peer):
        return pltpu.make_async_remote_copy(
            src_ref=dst, dst_ref=dst,
            send_sem=send_sem.at[kind, peer], recv_sem=recv_sem.at[kind, peer],
            device_id={"table": peer}, device_id_type=MESH,
        )

    peers = [lax.rem(me + d, n) for d in range(1, n)]
    for peer in peers:
        exchange(0, ids_send.at[peer], ids.at[rep, me], peer).start()
        exchange(1, grad_send.at[peer], grads.at[rep, me], peer).start()
    for peer in peers:
        exchange(2, mig_send.at[peer], comb.at[blocks + me], peer).start()
    ids[rep, me] = ids_send[me]
    grads[rep, me] = grad_send[me]

    comb[0:blocks, 0:brows, :] = table[...]
    comb[0:blocks, brows:, :] = jnp.zeros((blocks, 8, dim), jnp.float32)
    comb[blocks + me] = jnp.zeros((brows + 8, dim), jnp.float32)
    for j in range(blocks):
        comb[j, brows : brows + 1, 0:brows] = accum[j : j + 1, :]

    for peer in peers:
        arrival(0, ids.at[rep, peer], peer).wait_recv()
        arrival(1, grads.at[rep, peer], peer).wait_recv()

    def hop(kind, way, origin):
        buffer = ids if kind == 0 else grads
        return pltpu.make_async_remote_copy(
            src_ref=buffer.at[origin], dst_ref=buffer.at[origin],
            send_sem=zsend_sem.at[way, kind, origin], recv_sem=zrecv_sem.at[kind, origin],
            device_id={"batch": rep + 1 - 2 * way}, device_id_type=MESH,
        )

    def send_on(way, origin):
        for kind in range(2):
            hop(kind, way, origin).start()

    @pl.when(has_up)
    def _():
        send_on(0, rep)

    @pl.when(has_down)
    def _():
        send_on(1, rep)

    for peer in peers:
        arrival(2, comb.at[blocks + peer], peer).wait_recv()

    row_id = lax.broadcasted_iota(jnp.int32, (brows, 128), 0)

    def counts_of(origin):
        places, counts = [], []
        for g in range(groups):
            named = ids[origin, g * per_group]
            for s in range(1, per_group):
                named = named + ids[origin, g * per_group + s]
            named = named.astype(jnp.int32) - 1
            places.append(jnp.right_shift(named[0:1, :], (brows - 1).bit_length()))
            rows = jnp.bitwise_and(named, brows - 1)
            count = jnp.zeros((brows, 128), jnp.float32)
            for k in range(rows.shape[0]):
                count = count + (rows[k : k + 1, :] == row_id).astype(jnp.float32)
            counts.append(count)
        return jnp.concatenate(places, axis=1), jnp.concatenate(counts, axis=1)

    def chosen(places, counts, first):
        return jnp.concatenate(
            [
                jnp.where(places == first + b, counts, 0.0).astype(jnp.bfloat16)
                for b in range(step_blocks)
            ],
            axis=0,
        )

    span = step_blocks * brows

    def copy_moved(j, carry):
        moved_hl[pl.ds(pl.multiple_of(j * brows, brows), brows), :] = split_halves(
            comb[source[j], 0:brows, :]
        )
        return carry

    lax.fori_loop(0, blocks, copy_moved, 0)

    pool_part[...] = jnp.zeros_like(pool_part)
    places, counts = counts_of(rep)
    gradients = split_halves(grads[rep].reshape(slots, dim))

    def own_step(i, carry):
        hits = chosen(places, counts, i * step_blocks)
        where = pl.ds(pl.multiple_of(i * span, span), span)
        total[where, :] = jnp.dot(hits, gradients, preferred_element_type=jnp.float32)
        both = lax.dot_general(
            hits, moved_hl[where, :], (((0,), (0,)), ((), ())),
            preferred_element_type=jnp.float32,
        )
        pool_part[...] += (both[:, :dim] + both[:, dim:]).reshape(n, cap, dim)
        return carry

    lax.fori_loop(0, blocks // step_blocks, own_step, 0)

    def give_back(peer):
        return pltpu.make_async_remote_copy(
            src_ref=pool_part.at[peer], dst_ref=pool_back.at[me],
            send_sem=psend_sem.at[peer], recv_sem=precv_sem.at[me],
            device_id={"table": peer}, device_id_type=MESH,
        )

    def given_back(peer):
        return pltpu.make_async_remote_copy(
            src_ref=pool_part.at[peer], dst_ref=pool_back.at[peer],
            send_sem=psend_sem.at[peer], recv_sem=precv_sem.at[peer],
            device_id={"table": peer}, device_id_type=MESH,
        )

    for peer in peers:
        give_back(peer).start()
    pool_back[me] = pool_part[me]

    def add_origin(origin):
        places, counts = counts_of(origin)
        gradients = split_halves(grads[origin].reshape(slots, dim))

        def step(i, carry):
            hits = chosen(places, counts, i * step_blocks)
            where = pl.ds(pl.multiple_of(i * span, span), span)
            total[where, :] += jnp.dot(hits, gradients, preferred_element_type=jnp.float32)
            return carry

        lax.fori_loop(0, blocks // step_blocks, step, 0)

    def far_step(h, carry):
        below = rep - h
        above = rep + h

        @pl.when(below >= 0)
        def _():
            for kind in range(2):
                hop(kind, 0, below).wait_recv()

            @pl.when(has_up)
            def _():
                send_on(0, below)

        @pl.when(above < reps)
        def _():
            for kind in range(2):
                hop(kind, 1, above).wait_recv()

            @pl.when(has_down)
            def _():
                send_on(1, above)

        @pl.when(below >= 0)
        def _():
            add_origin(below)

        @pl.when(above < reps)
        def _():
            add_origin(above)

        return carry

    lax.fori_loop(1, reps, far_step, 0)

    eye = lax.broadcasted_iota(jnp.int32, (brows, brows), 0) == lax.broadcasted_iota(
        jnp.int32, (brows, brows), 1
    )

    def update(j, carry):
        where = pl.ds(pl.multiple_of(j * brows, brows), brows)
        both = total[where, :]
        row_grad = both[:, :dim] + both[:, dim:]
        at = source[j]
        old = comb[at, brows : brows + 1, 0:brows]
        old = jnp.sum(jnp.where(eye, old, 0.0), axis=1, keepdims=True)
        new = old + jnp.mean(row_grad * row_grad, axis=1, keepdims=True)
        table_out[j] = comb[at, 0:brows, :] - (LEARN_RATE * row_grad) / (jnp.sqrt(new) + EPSILON)
        accum_out[pl.ds(j, 1), :] = jnp.sum(jnp.where(eye, new, 0.0), axis=0, keepdims=True)
        return carry

    lax.fori_loop(0, blocks, update, 0)

    for peer in peers:
        given_back(peer).wait_recv()
    back = (
        lax.broadcasted_iota(jnp.int32, (samples, slots), 1) == bucket_col[...]
    ).astype(jnp.float32)
    pooled_out[...] = jnp.dot(
        back, pool_back[...].reshape(slots, dim), precision=EXACT,
        preferred_element_type=jnp.float32,
    )

    for peer in peers:
        exchange(0, ids_send.at[peer], ids.at[rep, me], peer).wait_send()
        exchange(1, grad_send.at[peer], grads.at[rep, me], peer).wait_send()
        exchange(2, mig_send.at[peer], comb.at[blocks + me], peer).wait_send()
        give_back(peer).wait_send()

    def drain(origin, carry):
        @pl.when(jnp.logical_and(has_up, origin <= rep))
        def _():
            for kind in range(2):
                hop(kind, 0, origin).wait_send()

        @pl.when(jnp.logical_and(has_down, origin >= rep))
        def _():
            for kind in range(2):
                hop(kind, 1, origin).wait_send()

        return carry

    lax.fori_loop(0, reps, drain, 0)


def gather_kernel(
    n, reps, cap,
    picked, source, bucket_col, lane_col, rows_t, named_t, table, accum, grad,
    pooled_out, table_out, accum_out,
    comb, mig_send, ids_send, units, ids, moved_hl, total, pool_part, pool_back,
    send_sem, recv_sem, zsend_sem, zrecv_sem, usend_sem, urecv_sem, psend_sem, precv_sem,
):
    me = lax.axis_index("table")
    rep = lax.axis_index("batch")
    blocks, brows, dim = table.shape
    samples = grad.shape[0]
    slots = n * cap
    groups = slots // 128
    per_group = 128 // cap
    has_up = rep < reps - 1
    has_down = rep > 0
    step_blocks = 4 if blocks % 4 == 0 else 1
    span = step_blocks * brows

    barrier = pltpu.get_barrier_semaphore()
    for d in range(1, n):
        pl.semaphore_signal(
            barrier, inc=1, device_id={"table": lax.rem(me + d, n)}, device_id_type=MESH
        )

    @pl.when(has_up)
    def _():
        pl.semaphore_signal(barrier, inc=1, device_id={"batch": rep + 1}, device_id_type=MESH)

    @pl.when(has_down)
    def _():
        pl.semaphore_signal(barrier, inc=1, device_id={"batch": rep - 1}, device_id_type=MESH)

    units[rep, me, 0:samples, :] = grad[...]
    units[rep, me, samples:, :] = named_t[...]
    lanes = (
        lax.broadcasted_iota(jnp.int32, (samples, n * 128), 1) == lane_col[...]
    ).astype(jnp.float32)
    sent_ids = jnp.dot(rows_t[...], lanes, precision=EXACT, preferred_element_type=jnp.float32)
    for d in range(n):
        ids_send[d] = sent_ids[:, d * 128 : (d + 1) * 128]
        mig_send[d, 0:brows, :] = table[picked[d]]
        mig_send[d, brows:, :] = jnp.zeros((8, dim), jnp.float32)
        mig_send[d, brows : brows + 1, 0:brows] = accum[pl.ds(picked[d], 1), :]

    neighbours = jnp.where(has_up, 1, 0) + jnp.where(has_down, 1, 0)
    pl.semaphore_wait(barrier, n - 1 + neighbours)

    def exchange(kind, src, dst, peer):
        return pltpu.make_async_remote_copy(
            src_ref=src, dst_ref=dst,
            send_sem=send_sem.at[kind, peer], recv_sem=recv_sem.at[kind, me],
            device_id={"table": peer}, device_id_type=MESH,
        )

    def arrival(kind, dst, peer):
        return pltpu.make_async_remote_copy(
            src_ref=dst, dst_ref=dst,
            send_sem=send_sem.at[kind, peer], recv_sem=recv_sem.at[kind, peer],
            device_id={"table": peer}, device_id_type=MESH,
        )

    peers = [lax.rem(me + d, n) for d in range(1, n)]

    parity = me % 2
    across = me + 4 - 8 * ((me // 4) % 2)
    along = me + 2 - 4 * ((me // 2) % 2)
    first = across + parity * (along - across)
    second = along + parity * (across - along)
    beside = me + 1 - 2 * parity
    corner = first + second - me

    def hop(way, origin):
        return pltpu.make_async_remote_copy(
            src_ref=units.at[origin, me], dst_ref=units.at[origin, me],
            send_sem=zsend_sem.at[way, origin], recv_sem=zrecv_sem.at[origin],
            device_id={"batch": rep + 1 - 2 * way}, device_id_type=MESH,
        )

    def relay(stage, origin, unit):
        return pltpu.make_async_remote_copy(
            src_ref=units.at[origin, unit], dst_ref=units.at[origin, unit],
            send_sem=usend_sem.at[stage, origin, unit], recv_sem=urecv_sem.at[origin, unit],
            device_id={"table": (first, second, beside)[stage]}, device_id_type=MESH,
        )

    def over(step, body):
        if step == 0:
            body(rep, None)
            return

        @pl.when(rep - step >= 0)
        def _():
            body(rep - step, 0)

        @pl.when(rep + step < reps)
        def _():
            body(rep + step, 1)

    def enter(origin, way):
        if way is not None:
            hop(way, origin).wait_recv()
        if way != 1:
            @pl.when(has_up)
            def _():
                hop(0, origin).start()
        if way != 0:
            @pl.when(has_down)
            def _():
                hop(1, origin).start()
        for stage in range(3):
            relay(stage, origin, me).start()

    def from_first(origin, way):
        relay(0, origin, first).wait_recv()
        relay(1, origin, first).start()
        relay(2, origin, first).start()

    def from_second(origin, way):
        for unit in (second, corner):
            relay(1, origin, unit).wait_recv()
            relay(2, origin, unit).start()

    row_id = lax.broadcasted_iota(jnp.int32, (brows, 128), 0)

    def count_rows(named):
        rows = jnp.bitwise_and(named, brows - 1)
        count = jnp.zeros((brows, 128), jnp.float32)
        for k in range(rows.shape[0]):
            count = count + (rows[k : k + 1, :] == row_id).astype(jnp.float32)
        return jnp.right_shift(named[0:1, :], (brows - 1).bit_length()), count

    def chosen(places, counts, start):
        return jnp.concatenate(
            [
                jnp.where(places == start + b, counts, 0.0).astype(jnp.bfloat16)
                for b in range(step_blocks)
            ],
            axis=0,
        )

    def joined(pairs):
        return (
            jnp.concatenate([p for p, _ in pairs], axis=1),
            jnp.concatenate([c for _, c in pairs], axis=1),
        )

    def add_units(origin, which):
        places, counts = joined(
            [
                count_rows(units[origin, u, samples:, :].astype(jnp.int32) - me * (blocks * brows))
                for u in which
            ]
        )
        gradients = jnp.concatenate(
            [split_halves(units[origin, u, 0:samples, :]) for u in which], axis=0
        )

        def step(i, carry):
            hits = chosen(places, counts, i * step_blocks)
            where = pl.ds(pl.multiple_of(i * span, span), span)
            total[where, :] += jnp.dot(hits, gradients, preferred_element_type=jnp.float32)
            return carry

        lax.fori_loop(0, blocks // step_blocks, step, 0)

    def finish_near(origin, way):
        add_units(origin, (me, first, second, corner))

    beyond = [u + 1 - 2 * parity for u in (me, first, second, corner)]

    def finish_far(origin, way):
        for unit in beyond:
            relay(2, origin, unit).wait_recv()
        add_units(origin, beyond)

    over(0, enter)
    for peer in peers:
        exchange(0, ids_send.at[peer], ids.at[me], peer).start()
    for peer in peers:
        exchange(1, mig_send.at[peer], comb.at[blocks + me], peer).start()
    ids[me] = ids_send[me]
    comb[0:blocks, 0:brows, :] = table[...]
    comb[0:blocks, brows:, :] = jnp.zeros((blocks, 8, dim), jnp.float32)
    comb[blocks + me] = jnp.zeros((brows + 8, dim), jnp.float32)
    for j in range(blocks):
        comb[j, brows : brows + 1, 0:brows] = accum[j : j + 1, :]
    total[...] = jnp.zeros_like(total)
    pool_part[...] = jnp.zeros_like(pool_part)

    if reps > 1:
        over(1, enter)
    over(0, from_first)

    for peer in peers:
        arrival(0, ids.at[peer], peer).wait_recv()
    for peer in peers:
        arrival(1, comb.at[blocks + peer], peer).wait_recv()
    pairs = []
    for g in range(groups):
        named = ids[g * per_group]
        for s in range(1, per_group):
            named = named + ids[g * per_group + s]
        pairs.append(count_rows(named.astype(jnp.int32) - 1))
    asked, asked_counts = joined(pairs)

    def copy_moved(j, carry):
        moved_hl[pl.ds(pl.multiple_of(j * brows, brows), brows), :] = split_halves(
            comb[source[j], 0:brows, :]
        )
        return carry

    lax.fori_loop(0, blocks, copy_moved, 0)

    def pool_step(i, carry):
        where = pl.ds(pl.multiple_of(i * span, span), span)
        both = lax.dot_general(
            chosen(asked, asked_counts, i * step_blocks), moved_hl[where, :],
            (((0,), (0,)), ((), ())), preferred_element_type=jnp.float32,
        )
        pool_part[...] += (both[:, :dim] + both[:, dim:]).reshape(n, cap, dim)
        return carry

    lax.fori_loop(0, blocks // step_blocks, pool_step, 0)

    def give_back(peer, owner):
        return pltpu.make_async_remote_copy(
            src_ref=pool_part.at[peer], dst_ref=pool_back.at[owner],
            send_sem=psend_sem.at[peer], recv_sem=precv_sem.at[owner],
            device_id={"table": peer}, device_id_type=MESH,
        )

    for peer in peers:
        give_back(peer, me).start()
    pool_back[me] = pool_part[me]

    for step in range(2, reps + 4):
        for lag, body in ((0, enter), (1, from_first), (2, from_second)):
            if 0 <= step - lag < reps:
                over(step - lag, body)
        for lag, body in ((2, finish_near), (3, finish_far)):
            if 0 <= step - lag < reps:
                over(step - lag, body)

    eye = lax.broadcasted_iota(jnp.int32, (brows, brows), 0) == lax.broadcasted_iota(
        jnp.int32, (brows, brows), 1
    )

    def update(j, carry):
        where = pl.ds(pl.multiple_of(j * brows, brows), brows)
        both = total[where, :]
        row_grad = both[:, :dim] + both[:, dim:]
        at = source[j]
        old = comb[at, brows : brows + 1, 0:brows]
        old = jnp.sum(jnp.where(eye, old, 0.0), axis=1, keepdims=True)
        new = old + jnp.mean(row_grad * row_grad, axis=1, keepdims=True)
        table_out[j] = comb[at, 0:brows, :] - (LEARN_RATE * row_grad) / (jnp.sqrt(new) + EPSILON)
        accum_out[pl.ds(j, 1), :] = jnp.sum(jnp.where(eye, new, 0.0), axis=0, keepdims=True)
        return carry

    lax.fori_loop(0, blocks, update, 0)

    for peer in peers:
        give_back(peer, peer).wait_recv()
    back = (
        lax.broadcasted_iota(jnp.int32, (samples, slots), 1) == bucket_col[...]
    ).astype(jnp.float32)
    pooled_out[...] = jnp.dot(
        back, pool_back[...].reshape(slots, dim), precision=EXACT,
        preferred_element_type=jnp.float32,
    )

    for peer in peers:
        exchange(0, ids_send.at[peer], ids.at[me], peer).wait_send()
        exchange(1, mig_send.at[peer], comb.at[blocks + me], peer).wait_send()
        give_back(peer, me).wait_send()

    def drain(origin, carry):
        @pl.when(jnp.logical_and(has_up, origin <= rep))
        def _():
            hop(0, origin).wait_send()

        @pl.when(jnp.logical_and(has_down, origin >= rep))
        def _():
            hop(1, origin).wait_send()

        for stage, sent in ((0, (me,)), (1, (me, first)), (2, (me, first, second, corner))):
            for unit in sent:
                relay(stage, origin, unit).wait_send()
        return carry

    lax.fori_loop(0, reps, drain, 0)


def per_device(table_rows, accum, plan_dest, plan_slot, bag_block, bag_rows, grad_pooled):
    blocks, brows, dim = table_rows.shape
    n = lax.axis_size("table")
    reps = lax.axis_size("batch")
    me = lax.axis_index("table")
    moving = plan_dest.shape[1]
    samples, pool = bag_rows.shape
    cap = 4 * samples // n
    owners = jnp.arange(n, dtype=jnp.int32)

    targets = plan_dest.reshape(-1)
    sources = jnp.arange(n * moving, dtype=jnp.int32) // moving
    earlier = (targets[:, None] == targets[None, :]) & (sources[None, :] < sources[:, None])
    rank = jnp.sum(earlier.astype(jnp.int32), axis=1)
    landing_at = targets * moving + rank
    every = jnp.arange(n * moving, dtype=jnp.int32)
    landing = jnp.sum(
        jnp.where(landing_at[:, None] == every[None, :], plan_slot.reshape(-1)[None, :], 0), axis=1
    )
    old_spot = sources * blocks + plan_slot.reshape(-1)
    new_spot = targets * blocks + landing

    mine = sources == me
    picked = jnp.sum(
        jnp.where(
            mine[None, :] & (targets[None, :] == owners[:, None]), plan_slot.reshape(-1)[None, :], 0
        ),
        axis=1,
    )
    spots = me * blocks + jnp.arange(blocks, dtype=jnp.int32)
    comes = new_spot[None, :] == spots[:, None]
    source = jnp.where(
        jnp.any(comes, axis=1),
        blocks + jnp.sum(jnp.where(comes, sources[None, :], 0), axis=1),
        jnp.arange(blocks, dtype=jnp.int32),
    )

    moves = bag_block[:, None] == old_spot[None, :]
    read = bag_block + jnp.sum(jnp.where(moves, (new_spot - old_spot)[None, :], 0), axis=1)
    owner = read // blocks
    order = jnp.arange(samples, dtype=jnp.int32)
    slot = jnp.sum(
        ((owner[:, None] == owner[None, :]) & (order[None, :] < order[:, None])).astype(jnp.int32),
        axis=1,
    )
    bucket = owner * cap + slot
    lane = owner * 128 + (me % (128 // cap)) * cap + slot
    rows_t = (((read - owner * blocks) * brows)[None, :] + bag_rows.T + 1).astype(jnp.float32)

    vmem = pl.BlockSpec(memory_space=pltpu.VMEM)
    smem = pl.BlockSpec(memory_space=pltpu.SMEM)
    slots = n * cap
    f32 = jnp.float32
    out_shape = (
        jax.ShapeDtypeStruct((samples, dim), f32),
        jax.ShapeDtypeStruct((blocks, brows, dim), f32),
        jax.ShapeDtypeStruct((blocks, brows), f32),
    )
    unit_bytes = 4 * (samples + pool) * dim
    if n == 8 and pool == 8 and samples == 128 and n * reps * unit_bytes <= 16 * 1024 * 1024:
        named_t = ((read * brows)[None, :] + bag_rows.T).astype(f32)
        return pl.pallas_call(
            functools.partial(gather_kernel, n, reps, cap),
            out_shape=out_shape,
            in_specs=[smem] * 2 + [vmem] * 7,
            out_specs=(vmem, vmem, vmem),
            scratch_shapes=[
                pltpu.VMEM((blocks + n, brows + 8, dim), f32),
                pltpu.VMEM((n, brows + 8, dim), f32),
                pltpu.VMEM((n, pool, 128), f32),
                pltpu.VMEM((reps, n, samples + pool, dim), f32),
                pltpu.VMEM((n, pool, 128), f32),
                pltpu.VMEM((blocks * brows, 2 * dim), jnp.bfloat16),
                pltpu.VMEM((blocks * brows, 2 * dim), f32),
                pltpu.VMEM((n, cap, dim), f32),
                pltpu.VMEM((n, cap, dim), f32),
                pltpu.SemaphoreType.DMA((2, n)),
                pltpu.SemaphoreType.DMA((2, n)),
                pltpu.SemaphoreType.DMA((2, reps)),
                pltpu.SemaphoreType.DMA((reps,)),
                pltpu.SemaphoreType.DMA((3, reps, n)),
                pltpu.SemaphoreType.DMA((reps, n)),
                pltpu.SemaphoreType.DMA((n,)),
                pltpu.SemaphoreType.DMA((n,)),
            ],
            compiler_params=pltpu.CompilerParams(
                collective_id=1, has_side_effects=True, vmem_limit_bytes=48 * 1024 * 1024
            ),
        )(
            picked, source, bucket[:, None], lane[:, None], rows_t, named_t,
            table_rows, accum, grad_pooled,
        )
    return pl.pallas_call(
        functools.partial(bucket_kernel, n, reps, cap),
        out_shape=out_shape,
        in_specs=[smem] * 2 + [vmem] * 7,
        out_specs=(vmem, vmem, vmem),
        scratch_shapes=[
            pltpu.VMEM((blocks + n, brows + 8, dim), f32),
            pltpu.VMEM((n, brows + 8, dim), f32),
            pltpu.VMEM((n, pool, 128), f32),
            pltpu.VMEM((n, cap, dim), f32),
            pltpu.VMEM((reps, n, cap, dim), f32),
            pltpu.VMEM((reps, n, pool, 128), f32),
            pltpu.VMEM((blocks * brows, 2 * dim), jnp.bfloat16),
            pltpu.VMEM((blocks * brows, 2 * dim), f32),
            pltpu.VMEM((n, cap, dim), f32),
            pltpu.VMEM((n, cap, dim), f32),
            pltpu.SemaphoreType.DMA((3, n)),
            pltpu.SemaphoreType.DMA((3, n)),
            pltpu.SemaphoreType.DMA((2, 2, reps)),
            pltpu.SemaphoreType.DMA((2, reps)),
            pltpu.SemaphoreType.DMA((n,)),
            pltpu.SemaphoreType.DMA((n,)),
        ],
        compiler_params=pltpu.CompilerParams(
            collective_id=0, has_side_effects=True, vmem_limit_bytes=48 * 1024 * 1024
        ),
    )(
        picked, source, bucket[None, :], bucket[:, None], lane[:, None], rows_t,
        table_rows, accum, grad_pooled,
    )


def solution(mesh):
    return jax.shard_map(
        per_device,
        mesh=mesh,
        in_specs=(
            P("table", None, None),
            P("table", None),
            P(),
            P(),
            P(("table", "batch")),
            P(("table", "batch"), None),
            P(("table", "batch"), None),
        ),
        out_specs=(P(("table", "batch"), None), P("table", None, None), P("table", None)),
        check_vma=False,
    )
```

```python
import functools

import jax
import jax.numpy as jnp
from jax import lax
from jax.experimental import pallas as pl
from jax.experimental.pallas import tpu as pltpu
from jax.sharding import PartitionSpec as P

LEARN_RATE = 0.3
EPSILON = 1e-08
MESH = pl.DeviceIdType.MESH
EXACT = lax.Precision.HIGHEST


def split_halves(values):
    high = values.astype(jnp.bfloat16)
    low = (values - high.astype(jnp.float32)).astype(jnp.bfloat16)
    return jnp.concatenate([high, low], axis=1)


def bucket_kernel(
    n, reps, cap,
    picked, source, bucket_row, bucket_col, lane_col, rows_t, table, accum, grad,
    pooled_out, table_out, accum_out,
    comb, mig_send, ids_send, grad_send, grads, ids, moved_hl, total, pool_part, pool_back,
    send_sem, recv_sem, zsend_sem, zrecv_sem, psend_sem, precv_sem,
):
    me = lax.axis_index("table")
    rep = lax.axis_index("batch")
    blocks, brows, dim = table.shape
    samples = grad.shape[0]
    slots = n * cap
    groups = slots // 128
    per_group = 128 // cap
    has_up = rep < reps - 1
    has_down = rep > 0
    step_blocks = 4 if blocks % 4 == 0 else 1

    barrier = pltpu.get_barrier_semaphore()
    for d in range(1, n):
        pl.semaphore_signal(
            barrier, inc=1, device_id={"table": lax.rem(me + d, n)}, device_id_type=MESH
        )

    @pl.when(has_up)
    def _():
        pl.semaphore_signal(barrier, inc=1, device_id={"batch": rep + 1}, device_id_type=MESH)

    @pl.when(has_down)
    def _():
        pl.semaphore_signal(barrier, inc=1, device_id={"batch": rep - 1}, device_id_type=MESH)

    place = (
        lax.broadcasted_iota(jnp.int32, (slots, samples), 0) == bucket_row[...]
    ).astype(jnp.float32)
    sent = jnp.dot(place, grad[...], precision=EXACT, preferred_element_type=jnp.float32)
    grad_send[...] = sent.reshape(n, cap, dim)
    lanes = (
        lax.broadcasted_iota(jnp.int32, (samples, n * 128), 1) == lane_col[...]
    ).astype(jnp.float32)
    sent_ids = jnp.dot(rows_t[...], lanes, precision=EXACT, preferred_element_type=jnp.float32)
    for d in range(n):
        ids_send[d] = sent_ids[:, d * 128 : (d + 1) * 128]

    for d in range(n):
        mig_send[d, 0:brows, :] = table[picked[d]]
        mig_send[d, brows:, :] = jnp.zeros((8, dim), jnp.float32)
        mig_send[d, brows : brows + 1, 0:brows] = accum[pl.ds(picked[d], 1), :]

    neighbours = jnp.where(has_up, 1, 0) + jnp.where(has_down, 1, 0)
    pl.semaphore_wait(barrier, n - 1 + neighbours)

    def exchange(kind, src, dst, peer):
        return pltpu.make_async_remote_copy(
            src_ref=src, dst_ref=dst,
            send_sem=send_sem.at[kind, peer], recv_sem=recv_sem.at[kind, me],
            device_id={"table": peer}, device_id_type=MESH,
        )

    def arrival(kind, dst, peer):
        return pltpu.make_async_remote_copy(
            src_ref=dst, dst_ref=dst,
            send_sem=send_sem.at[kind, peer], recv_sem=recv_sem.at[kind, peer],
            device_id={"table": peer}, device_id_type=MESH,
        )

    peers = [lax.rem(me + d, n) for d in range(1, n)]
    for peer in peers:
        exchange(0, ids_send.at[peer], ids.at[rep, me], peer).start()
        exchange(1, grad_send.at[peer], grads.at[rep, me], peer).start()
    for peer in peers:
        exchange(2, mig_send.at[peer], comb.at[blocks + me], peer).start()
    ids[rep, me] = ids_send[me]
    grads[rep, me] = grad_send[me]

    comb[0:blocks, 0:brows, :] = table[...]
    comb[0:blocks, brows:, :] = jnp.zeros((blocks, 8, dim), jnp.float32)
    comb[blocks + me] = jnp.zeros((brows + 8, dim), jnp.float32)
    for j in range(blocks):
        comb[j, brows : brows + 1, 0:brows] = accum[j : j + 1, :]

    for peer in peers:
        arrival(0, ids.at[rep, peer], peer).wait_recv()
        arrival(1, grads.at[rep, peer], peer).wait_recv()

    def hop(kind, way, origin):
        buffer = ids if kind == 0 else grads
        return pltpu.make_async_remote_copy(
            src_ref=buffer.at[origin], dst_ref=buffer.at[origin],
            send_sem=zsend_sem.at[way, kind, origin], recv_sem=zrecv_sem.at[kind, origin],
            device_id={"batch": rep + 1 - 2 * way}, device_id_type=MESH,
        )

    def send_on(way, origin):
        for kind in range(2):
            hop(kind, way, origin).start()

    @pl.when(has_up)
    def _():
        send_on(0, rep)

    @pl.when(has_down)
    def _():
        send_on(1, rep)

    for peer in peers:
        arrival(2, comb.at[blocks + peer], peer).wait_recv()

    row_id = lax.broadcasted_iota(jnp.int32, (brows, 128), 0)

    def counts_of(origin):
        places, counts = [], []
        for g in range(groups):
            named = ids[origin, g * per_group]
            for s in range(1, per_group):
                named = named + ids[origin, g * per_group + s]
            named = named.astype(jnp.int32) - 1
            places.append(jnp.right_shift(named[0:1, :], (brows - 1).bit_length()))
            rows = jnp.bitwise_and(named, brows - 1)
            count = jnp.zeros((brows, 128), jnp.float32)
            for k in range(rows.shape[0]):
                count = count + (rows[k : k + 1, :] == row_id).astype(jnp.float32)
            counts.append(count)
        return jnp.concatenate(places, axis=1), jnp.concatenate(counts, axis=1)

    def chosen(places, counts, first):
        return jnp.concatenate(
            [
                jnp.where(places == first + b, counts, 0.0).astype(jnp.bfloat16)
                for b in range(step_blocks)
            ],
            axis=0,
        )

    span = step_blocks * brows

    def copy_moved(j, carry):
        moved_hl[pl.ds(pl.multiple_of(j * brows, brows), brows), :] = split_halves(
            comb[source[j], 0:brows, :]
        )
        return carry

    lax.fori_loop(0, blocks, copy_moved, 0)

    pool_part[...] = jnp.zeros_like(pool_part)
    places, counts = counts_of(rep)
    gradients = split_halves(grads[rep].reshape(slots, dim))

    def own_step(i, carry):
        hits = chosen(places, counts, i * step_blocks)
        where = pl.ds(pl.multiple_of(i * span, span), span)
        total[where, :] = jnp.dot(hits, gradients, preferred_element_type=jnp.float32)
        both = lax.dot_general(
            hits, moved_hl[where, :], (((0,), (0,)), ((), ())),
            preferred_element_type=jnp.float32,
        )
        pool_part[...] += (both[:, :dim] + both[:, dim:]).reshape(n, cap, dim)
        return carry

    lax.fori_loop(0, blocks // step_blocks, own_step, 0)

    def give_back(peer):
        return pltpu.make_async_remote_copy(
            src_ref=pool_part.at[peer], dst_ref=pool_back.at[me],
            send_sem=psend_sem.at[peer], recv_sem=precv_sem.at[me],
            device_id={"table": peer}, device_id_type=MESH,
        )

    def given_back(peer):
        return pltpu.make_async_remote_copy(
            src_ref=pool_part.at[peer], dst_ref=pool_back.at[peer],
            send_sem=psend_sem.at[peer], recv_sem=precv_sem.at[peer],
            device_id={"table": peer}, device_id_type=MESH,
        )

    for peer in peers:
        give_back(peer).start()
    pool_back[me] = pool_part[me]

    def add_origin(origin):
        places, counts = counts_of(origin)
        gradients = split_halves(grads[origin].reshape(slots, dim))

        def step(i, carry):
            hits = chosen(places, counts, i * step_blocks)
            where = pl.ds(pl.multiple_of(i * span, span), span)
            total[where, :] += jnp.dot(hits, gradients, preferred_element_type=jnp.float32)
            return carry

        lax.fori_loop(0, blocks // step_blocks, step, 0)

    def far_step(h, carry):
        below = rep - h
        above = rep + h

        @pl.when(below >= 0)
        def _():
            for kind in range(2):
                hop(kind, 0, below).wait_recv()

            @pl.when(has_up)
            def _():
                send_on(0, below)

        @pl.when(above < reps)
        def _():
            for kind in range(2):
                hop(kind, 1, above).wait_recv()

            @pl.when(has_down)
            def _():
                send_on(1, above)

        @pl.when(below >= 0)
        def _():
            add_origin(below)

        @pl.when(above < reps)
        def _():
            add_origin(above)

        return carry

    lax.fori_loop(1, reps, far_step, 0)

    eye = lax.broadcasted_iota(jnp.int32, (brows, brows), 0) == lax.broadcasted_iota(
        jnp.int32, (brows, brows), 1
    )

    def update(j, carry):
        where = pl.ds(pl.multiple_of(j * brows, brows), brows)
        both = total[where, :]
        row_grad = both[:, :dim] + both[:, dim:]
        at = source[j]
        old = comb[at, brows : brows + 1, 0:brows]
        old = jnp.sum(jnp.where(eye, old, 0.0), axis=1, keepdims=True)
        new = old + jnp.mean(row_grad * row_grad, axis=1, keepdims=True)
        table_out[j] = comb[at, 0:brows, :] - (LEARN_RATE * row_grad) / (jnp.sqrt(new) + EPSILON)
        accum_out[pl.ds(j, 1), :] = jnp.sum(jnp.where(eye, new, 0.0), axis=0, keepdims=True)
        return carry

    lax.fori_loop(0, blocks, update, 0)

    for peer in peers:
        given_back(peer).wait_recv()
    back = (
        lax.broadcasted_iota(jnp.int32, (samples, slots), 1) == bucket_col[...]
    ).astype(jnp.float32)
    pooled_out[...] = jnp.dot(
        back, pool_back[...].reshape(slots, dim), precision=EXACT,
        preferred_element_type=jnp.float32,
    )

    for peer in peers:
        exchange(0, ids_send.at[peer], ids.at[rep, me], peer).wait_send()
        exchange(1, grad_send.at[peer], grads.at[rep, me], peer).wait_send()
        exchange(2, mig_send.at[peer], comb.at[blocks + me], peer).wait_send()
        give_back(peer).wait_send()

    def drain(origin, carry):
        @pl.when(jnp.logical_and(has_up, origin <= rep))
        def _():
            for kind in range(2):
                hop(kind, 0, origin).wait_send()

        @pl.when(jnp.logical_and(has_down, origin >= rep))
        def _():
            for kind in range(2):
                hop(kind, 1, origin).wait_send()

        return carry

    lax.fori_loop(0, reps, drain, 0)


def gather_kernel(
    n, reps, cap,
    dest, slot, bag_block, bag_rows, accum, table, grad,
    pooled_out, table_out, accum_out,
    comb, mig_send, ids_send, units, ids, moved_hl, total, pool_part, pool_back,
    send_sem, recv_sem, zsend_sem, zrecv_sem, usend_sem, urecv_sem, psend_sem, precv_sem, load_sem, held,
):
    me = lax.axis_index("table")
    rep = lax.axis_index("batch")
    blocks, brows, dim = table.shape
    samples = grad.shape[0]
    slots = n * cap
    groups = slots // 128
    per_group = 128 // cap
    has_up = rep < reps - 1
    has_down = rep > 0
    step_blocks = 4 if blocks % 4 == 0 else 1
    span = step_blocks * brows

    barrier = pltpu.get_barrier_semaphore()
    for d in range(1, n):
        pl.semaphore_signal(
            barrier, inc=1, device_id={"table": lax.rem(me + d, n)}, device_id_type=MESH
        )

    @pl.when(has_up)
    def _():
        pl.semaphore_signal(barrier, inc=1, device_id={"batch": rep + 1}, device_id_type=MESH)

    @pl.when(has_down)
    def _():
        pl.semaphore_signal(barrier, inc=1, device_id={"batch": rep - 1}, device_id_type=MESH)

    load_grad = pltpu.make_async_copy(
        grad, units.at[rep, me, pl.ds(0, samples)], load_sem.at[0]
    )
    load_table = pltpu.make_async_copy(
        table, comb.at[pl.ds(0, blocks), pl.ds(0, brows)], load_sem.at[1]
    )
    load_held = pltpu.make_async_copy(table, held, load_sem.at[2])
    load_grad.start()
    load_held.start()
    load_table.start()

    f32 = jnp.float32
    unit_eye = lax.broadcasted_iota(jnp.int32, (samples, samples), 0) == lax.broadcasted_iota(
        jnp.int32, (samples, samples), 1
    )
    rows_t = lax.dot_general(
        bag_rows[...].astype(f32), unit_eye.astype(f32), (((0,), (0,)), ((), ())),
        precision=EXACT, preferred_element_type=f32,
    )
    named_t = (bag_block[...] * brows).astype(f32) + rows_t
    units[rep, me, samples:, :] = named_t
    load_grad.wait()

    neighbours = jnp.where(has_up, 1, 0) + jnp.where(has_down, 1, 0)
    pl.semaphore_wait(barrier, n - 1 + neighbours)

    def exchange(kind, src, dst, peer):
        return pltpu.make_async_remote_copy(
            src_ref=src, dst_ref=dst,
            send_sem=send_sem.at[kind, peer], recv_sem=recv_sem.at[kind, me],
            device_id={"table": peer}, device_id_type=MESH,
        )

    def arrival(kind, dst, peer):
        return pltpu.make_async_remote_copy(
            src_ref=dst, dst_ref=dst,
            send_sem=send_sem.at[kind, peer], recv_sem=recv_sem.at[kind, peer],
            device_id={"table": peer}, device_id_type=MESH,
        )

    peers = [lax.rem(me + d, n) for d in range(1, n)]

    parity = me % 2
    across = me + 4 - 8 * ((me // 4) % 2)
    along = me + 2 - 4 * ((me // 2) % 2)
    first = across + parity * (along - across)
    second = along + parity * (across - along)
    beside = me + 1 - 2 * parity
    corner = first + second - me

    def hop(way, origin):
        return pltpu.make_async_remote_copy(
            src_ref=units.at[origin, me], dst_ref=units.at[origin, me],
            send_sem=zsend_sem.at[way, origin], recv_sem=zrecv_sem.at[origin],
            device_id={"batch": rep + 1 - 2 * way}, device_id_type=MESH,
        )

    def relay(stage, origin, unit):
        return pltpu.make_async_remote_copy(
            src_ref=units.at[origin, unit], dst_ref=units.at[origin, unit],
            send_sem=usend_sem.at[stage, origin, unit], recv_sem=urecv_sem.at[origin, unit],
            device_id={"table": (first, second, beside)[stage]}, device_id_type=MESH,
        )

    def over(step, body):
        if step == 0:
            body(rep, None)
            return

        @pl.when(rep - step >= 0)
        def _():
            body(rep - step, 0)

        @pl.when(rep + step < reps)
        def _():
            body(rep + step, 1)

    def enter(origin, way):
        if way is not None:
            hop(way, origin).wait_recv()
        if way != 1:
            @pl.when(has_up)
            def _():
                hop(0, origin).start()
        if way != 0:
            @pl.when(has_down)
            def _():
                hop(1, origin).start()
        for stage in range(3):
            relay(stage, origin, me).start()

    def from_first(origin, way):
        relay(0, origin, first).wait_recv()
        relay(1, origin, first).start()
        relay(2, origin, first).start()

    def from_second(origin, way):
        for unit in (second, corner):
            relay(1, origin, unit).wait_recv()
            relay(2, origin, unit).start()

    row_id = lax.broadcasted_iota(jnp.int32, (brows, 128), 0)

    def count_rows(named):
        rows = jnp.bitwise_and(named, brows - 1)
        count = jnp.zeros((brows, 128), jnp.float32)
        for k in range(rows.shape[0]):
            count = count + (rows[k : k + 1, :] == row_id).astype(jnp.float32)
        return jnp.right_shift(named[0:1, :], (brows - 1).bit_length()), count

    def chosen(places, counts, start):
        return jnp.concatenate(
            [
                jnp.where(places == former(start + b), counts, 0.0).astype(jnp.bfloat16)
                for b in range(step_blocks)
            ],
            axis=0,
        )

    def joined(pairs):
        return (
            jnp.concatenate([p for p, _ in pairs], axis=1),
            jnp.concatenate([c for _, c in pairs], axis=1),
        )

    def add_units(origin, which):
        places, counts = joined(
            [
                count_rows(units[origin, u, samples:, :].astype(jnp.int32))
                for u in which
            ]
        )
        gradients = jnp.concatenate(
            [split_halves(units[origin, u, 0:samples, :]) for u in which], axis=0
        )

        def step(i, carry):
            hits = chosen(places, counts, i * step_blocks)
            where = pl.ds(pl.multiple_of(i * span, span), span)
            total[where, :] += jnp.dot(hits, gradients, preferred_element_type=jnp.float32)
            return carry

        lax.fori_loop(0, blocks // step_blocks, step, 0)

    def finish_near(origin, way):
        add_units(origin, (me, first, second, corner))

    beyond = [u + 1 - 2 * parity for u in (me, first, second, corner)]

    def finish_far(origin, way):
        for unit in beyond:
            relay(2, origin, unit).wait_recv()
        add_units(origin, beyond)

    over(0, enter)

    moving = dest.shape[1]
    count = jnp.int32(0)
    giver = [jnp.int32(0)] * moving
    given = [jnp.int32(0)] * moving
    for s in range(n):
        for k in range(moving):
            hit = dest[s, k] == me
            for r in range(moving):
                now = jnp.logical_and(hit, count == r)
                giver[r] = jnp.where(now, s, giver[r])
                given[r] = jnp.where(now, s * blocks + slot[s, k], given[r])
            count = count + jnp.where(hit, 1, 0)
    freed = [slot[me, r] for r in range(moving)]
    towards = [dest[me, r] for r in range(moving)]

    def source(j):
        at = j
        for r in range(moving):
            at = jnp.where(j == freed[r], blocks + giver[r], at)
        return at

    def former(j):
        at = me * blocks + j
        for r in range(moving):
            at = jnp.where(j == freed[r], given[r], at)
        return at

    owner = jnp.zeros((1, samples), jnp.int32)
    for t in range(1, n):
        owner = owner + (bag_block[...] >= t * blocks).astype(jnp.int32)
    for s in range(n):
        for k in range(moving):
            owner = jnp.where(bag_block[...] == s * blocks + slot[s, k], dest[s, k], owner)
    owner = owner.astype(f32)
    owner_col = jnp.sum(jnp.where(unit_eye, owner, 0.0), axis=1, keepdims=True)
    before = lax.broadcasted_iota(jnp.int32, (samples, samples), 1) < lax.broadcasted_iota(
        jnp.int32, (samples, samples), 0
    )
    within = jnp.sum(
        jnp.where(jnp.logical_and(owner_col == owner, before), 1.0, 0.0), axis=1, keepdims=True
    ).astype(jnp.int32)
    owner_col = owner_col.astype(jnp.int32)
    bucket_col = owner_col * cap + within
    lane_col = owner_col * 128 + (me % per_group) * cap + within
    lanes = (
        lax.broadcasted_iota(jnp.int32, (samples, n * 128), 1) == lane_col
    ).astype(f32)
    sent_ids = jnp.dot(named_t + 1.0, lanes, precision=EXACT, preferred_element_type=f32)
    for d in range(n):
        ids_send[d] = sent_ids[:, d * 128 : (d + 1) * 128]
    for peer in peers:
        exchange(0, ids_send.at[peer], ids.at[me], peer).start()
    load_held.wait()
    load_table.wait()
    for d in range(n):
        picked = jnp.int32(0)
        for r in range(moving):
            picked = jnp.where(towards[r] == d, freed[r], picked)
        mig_send[d, 0:brows, :] = held[picked]
        mig_send[d, brows:, :] = jnp.zeros((8, dim), f32)
        mig_send[d, brows : brows + 1, 0:brows] = accum[pl.ds(picked, 1), :]
    for peer in peers:
        exchange(1, mig_send.at[peer], comb.at[blocks + me], peer).start()
    ids[me] = ids_send[me]
    comb[0:blocks, brows:, :] = jnp.zeros((blocks, 8, dim), jnp.float32)
    comb[blocks + me] = jnp.zeros((brows + 8, dim), jnp.float32)
    for j in range(blocks):
        comb[j, brows : brows + 1, 0:brows] = accum[j : j + 1, :]
    total[...] = jnp.zeros_like(total)
    pool_part[...] = jnp.zeros_like(pool_part)

    if reps > 1:
        over(1, enter)
    over(0, from_first)

    for peer in peers:
        arrival(0, ids.at[peer], peer).wait_recv()
    for peer in peers:
        arrival(1, comb.at[blocks + peer], peer).wait_recv()
    pairs = []
    for g in range(groups):
        named = ids[g * per_group]
        for s in range(1, per_group):
            named = named + ids[g * per_group + s]
        pairs.append(count_rows(named.astype(jnp.int32) - 1))
    asked, asked_counts = joined(pairs)

    def copy_moved(j, carry):
        moved_hl[pl.ds(pl.multiple_of(j * brows, brows), brows), :] = split_halves(
            comb[source(j), 0:brows, :]
        )
        return carry

    lax.fori_loop(0, blocks, copy_moved, 0)

    def pool_step(i, carry):
        where = pl.ds(pl.multiple_of(i * span, span), span)
        both = lax.dot_general(
            chosen(asked, asked_counts, i * step_blocks), moved_hl[where, :],
            (((0,), (0,)), ((), ())), preferred_element_type=jnp.float32,
        )
        pool_part[...] += (both[:, :dim] + both[:, dim:]).reshape(n, cap, dim)
        return carry

    lax.fori_loop(0, blocks // step_blocks, pool_step, 0)

    def give_back(peer, owner):
        return pltpu.make_async_remote_copy(
            src_ref=pool_part.at[peer], dst_ref=pool_back.at[owner],
            send_sem=psend_sem.at[peer], recv_sem=precv_sem.at[owner],
            device_id={"table": peer}, device_id_type=MESH,
        )

    for peer in peers:
        give_back(peer, me).start()
    pool_back[me] = pool_part[me]

    for step in range(2, reps + 4):
        for lag, body in ((0, enter), (1, from_first), (2, from_second)):
            if 0 <= step - lag < reps:
                over(step - lag, body)
        for lag, body in ((2, finish_near), (3, finish_far)):
            if 0 <= step - lag < reps:
                over(step - lag, body)

    eye = lax.broadcasted_iota(jnp.int32, (brows, brows), 0) == lax.broadcasted_iota(
        jnp.int32, (brows, brows), 1
    )

    def update(j, carry):
        where = pl.ds(pl.multiple_of(j * brows, brows), brows)
        both = total[where, :]
        row_grad = both[:, :dim] + both[:, dim:]
        at = source(j)
        old = comb[at, brows : brows + 1, 0:brows]
        old = jnp.sum(jnp.where(eye, old, 0.0), axis=1, keepdims=True)
        new = old + jnp.mean(row_grad * row_grad, axis=1, keepdims=True)
        table_out[j] = comb[at, 0:brows, :] - (LEARN_RATE * row_grad) / (jnp.sqrt(new) + EPSILON)
        accum_out[pl.ds(j, 1), :] = jnp.sum(jnp.where(eye, new, 0.0), axis=0, keepdims=True)
        return carry

    lax.fori_loop(0, blocks, update, 0)

    for peer in peers:
        give_back(peer, peer).wait_recv()
    back = (
        lax.broadcasted_iota(jnp.int32, (samples, slots), 1) == bucket_col
    ).astype(jnp.float32)
    pooled_out[...] = jnp.dot(
        back, pool_back[...].reshape(slots, dim), precision=EXACT,
        preferred_element_type=jnp.float32,
    )

    for peer in peers:
        exchange(0, ids_send.at[peer], ids.at[me], peer).wait_send()
        exchange(1, mig_send.at[peer], comb.at[blocks + me], peer).wait_send()
        give_back(peer, me).wait_send()

    def drain(origin, carry):
        @pl.when(jnp.logical_and(has_up, origin <= rep))
        def _():
            hop(0, origin).wait_send()

        @pl.when(jnp.logical_and(has_down, origin >= rep))
        def _():
            hop(1, origin).wait_send()

        for stage, sent in ((0, (me,)), (1, (me, first)), (2, (me, first, second, corner))):
            for unit in sent:
                relay(stage, origin, unit).wait_send()
        return carry

    lax.fori_loop(0, reps, drain, 0)


def per_device(table_rows, accum, plan_dest, plan_slot, bag_block, bag_rows, grad_pooled):
    blocks, brows, dim = table_rows.shape
    n = lax.axis_size("table")
    reps = lax.axis_size("batch")
    me = lax.axis_index("table")
    moving = plan_dest.shape[1]
    samples, pool = bag_rows.shape
    cap = 4 * samples // n
    vmem = pl.BlockSpec(memory_space=pltpu.VMEM)
    smem = pl.BlockSpec(memory_space=pltpu.SMEM)
    slots = n * cap
    f32 = jnp.float32
    out_shape = (
        jax.ShapeDtypeStruct((samples, dim), f32),
        jax.ShapeDtypeStruct((blocks, brows, dim), f32),
        jax.ShapeDtypeStruct((blocks, brows), f32),
    )
    unit_bytes = 4 * (samples + pool) * dim
    if n == 8 and pool == 8 and samples == 128 and n * reps * unit_bytes <= 16 * 1024 * 1024:
        return pl.pallas_call(
            functools.partial(gather_kernel, n, reps, cap),
            out_shape=out_shape,
            in_specs=[smem] * 2 + [vmem] * 3 + [pl.BlockSpec(memory_space=pl.ANY)] * 2,
            out_specs=(vmem, vmem, vmem),
            scratch_shapes=[
                pltpu.VMEM((blocks + n, brows + 8, dim), f32),
                pltpu.VMEM((n, brows + 8, dim), f32),
                pltpu.VMEM((n, pool, 128), f32),
                pltpu.VMEM((reps, n, samples + pool, dim), f32),
                pltpu.VMEM((n, pool, 128), f32),
                pltpu.VMEM((blocks * brows, 2 * dim), jnp.bfloat16),
                pltpu.VMEM((blocks * brows, 2 * dim), f32),
                pltpu.VMEM((n, cap, dim), f32),
                pltpu.VMEM((n, cap, dim), f32),
                pltpu.SemaphoreType.DMA((2, n)),
                pltpu.SemaphoreType.DMA((2, n)),
                pltpu.SemaphoreType.DMA((2, reps)),
                pltpu.SemaphoreType.DMA((reps,)),
                pltpu.SemaphoreType.DMA((3, reps, n)),
                pltpu.SemaphoreType.DMA((reps, n)),
                pltpu.SemaphoreType.DMA((n,)),
                pltpu.SemaphoreType.DMA((n,)),
                pltpu.SemaphoreType.DMA((3,)),
                pltpu.VMEM((blocks, brows, dim), f32),
            ],
            compiler_params=pltpu.CompilerParams(
                collective_id=1, has_side_effects=True, vmem_limit_bytes=48 * 1024 * 1024
            ),
        )(
            plan_dest, plan_slot, bag_block[None, :], bag_rows, accum, table_rows, grad_pooled,
        )

    owners = jnp.arange(n, dtype=jnp.int32)

    targets = plan_dest.reshape(-1)
    sources = jnp.arange(n * moving, dtype=jnp.int32) // moving
    earlier = (targets[:, None] == targets[None, :]) & (sources[None, :] < sources[:, None])
    rank = jnp.sum(earlier.astype(jnp.int32), axis=1)
    landing_at = targets * moving + rank
    every = jnp.arange(n * moving, dtype=jnp.int32)
    landing = jnp.sum(
        jnp.where(landing_at[:, None] == every[None, :], plan_slot.reshape(-1)[None, :], 0), axis=1
    )
    old_spot = sources * blocks + plan_slot.reshape(-1)
    new_spot = targets * blocks + landing

    mine = sources == me
    picked = jnp.sum(
        jnp.where(
            mine[None, :] & (targets[None, :] == owners[:, None]), plan_slot.reshape(-1)[None, :], 0
        ),
        axis=1,
    )
    spots = me * blocks + jnp.arange(blocks, dtype=jnp.int32)
    comes = new_spot[None, :] == spots[:, None]
    source = jnp.where(
        jnp.any(comes, axis=1),
        blocks + jnp.sum(jnp.where(comes, sources[None, :], 0), axis=1),
        jnp.arange(blocks, dtype=jnp.int32),
    )

    moves = bag_block[:, None] == old_spot[None, :]
    read = bag_block + jnp.sum(jnp.where(moves, (new_spot - old_spot)[None, :], 0), axis=1)
    owner = read // blocks
    order = jnp.arange(samples, dtype=jnp.int32)
    slot = jnp.sum(
        ((owner[:, None] == owner[None, :]) & (order[None, :] < order[:, None])).astype(jnp.int32),
        axis=1,
    )
    bucket = owner * cap + slot
    lane = owner * 128 + (me % (128 // cap)) * cap + slot
    rows_t = (((read - owner * blocks) * brows)[None, :] + bag_rows.T + 1).astype(jnp.float32)

    return pl.pallas_call(
        functools.partial(bucket_kernel, n, reps, cap),
        out_shape=out_shape,
        in_specs=[smem] * 2 + [vmem] * 7,
        out_specs=(vmem, vmem, vmem),
        scratch_shapes=[
            pltpu.VMEM((blocks + n, brows + 8, dim), f32),
            pltpu.VMEM((n, brows + 8, dim), f32),
            pltpu.VMEM((n, pool, 128), f32),
            pltpu.VMEM((n, cap, dim), f32),
            pltpu.VMEM((reps, n, cap, dim), f32),
            pltpu.VMEM((reps, n, pool, 128), f32),
            pltpu.VMEM((blocks * brows, 2 * dim), jnp.bfloat16),
            pltpu.VMEM((blocks * brows, 2 * dim), f32),
            pltpu.VMEM((n, cap, dim), f32),
            pltpu.VMEM((n, cap, dim), f32),
            pltpu.SemaphoreType.DMA((3, n)),
            pltpu.SemaphoreType.DMA((3, n)),
            pltpu.SemaphoreType.DMA((2, 2, reps)),
            pltpu.SemaphoreType.DMA((2, reps)),
            pltpu.SemaphoreType.DMA((n,)),
            pltpu.SemaphoreType.DMA((n,)),
        ],
        compiler_params=pltpu.CompilerParams(
            collective_id=0, has_side_effects=True, vmem_limit_bytes=48 * 1024 * 1024
        ),
    )(
        picked, source, bucket[None, :], bucket[:, None], lane[:, None], rows_t,
        table_rows, accum, grad_pooled,
    )


def solution(mesh):
    return jax.shard_map(
        per_device,
        mesh=mesh,
        in_specs=(
            P("table", None, None),
            P("table", None),
            P(),
            P(),
            P(("table", "batch")),
            P(("table", "batch"), None),
            P(("table", "batch"), None),
        ),
        out_specs=(P(("table", "batch"), None), P("table", None, None), P("table", None)),
        check_vma=False,
    )
```

```python
import functools

import jax
import jax.numpy as jnp
from jax import lax
from jax.experimental import pallas as pl
from jax.experimental.pallas import tpu as pltpu
from jax.sharding import PartitionSpec as P

LEARN_RATE = 0.3
EPSILON = 1e-08
MESH = pl.DeviceIdType.MESH
EXACT = lax.Precision.HIGHEST


def split_halves(values):
    high = values.astype(jnp.bfloat16)
    low = (values - high.astype(jnp.float32)).astype(jnp.bfloat16)
    return jnp.concatenate([high, low], axis=1)


def bucket_kernel(
    n, reps, cap,
    picked, source, bucket_row, bucket_col, lane_col, rows_t, table, accum, grad,
    pooled_out, table_out, accum_out,
    comb, mig_send, ids_send, grad_send, grads, ids, moved_hl, total, pool_part, pool_back,
    send_sem, recv_sem, zsend_sem, zrecv_sem, psend_sem, precv_sem,
):
    me = lax.axis_index("table")
    rep = lax.axis_index("batch")
    blocks, brows, dim = table.shape
    samples = grad.shape[0]
    slots = n * cap
    groups = slots // 128
    per_group = 128 // cap
    has_up = rep < reps - 1
    has_down = rep > 0
    step_blocks = 4 if blocks % 4 == 0 else 1

    barrier = pltpu.get_barrier_semaphore()
    for d in range(1, n):
        pl.semaphore_signal(
            barrier, inc=1, device_id={"table": lax.rem(me + d, n)}, device_id_type=MESH
        )

    @pl.when(has_up)
    def _():
        pl.semaphore_signal(barrier, inc=1, device_id={"batch": rep + 1}, device_id_type=MESH)

    @pl.when(has_down)
    def _():
        pl.semaphore_signal(barrier, inc=1, device_id={"batch": rep - 1}, device_id_type=MESH)

    place = (
        lax.broadcasted_iota(jnp.int32, (slots, samples), 0) == bucket_row[...]
    ).astype(jnp.float32)
    sent = jnp.dot(place, grad[...], precision=EXACT, preferred_element_type=jnp.float32)
    grad_send[...] = sent.reshape(n, cap, dim)
    lanes = (
        lax.broadcasted_iota(jnp.int32, (samples, n * 128), 1) == lane_col[...]
    ).astype(jnp.float32)
    sent_ids = jnp.dot(rows_t[...], lanes, precision=EXACT, preferred_element_type=jnp.float32)
    for d in range(n):
        ids_send[d] = sent_ids[:, d * 128 : (d + 1) * 128]

    for d in range(n):
        mig_send[d, 0:brows, :] = table[picked[d]]
        mig_send[d, brows:, :] = jnp.zeros((8, dim), jnp.float32)
        mig_send[d, brows : brows + 1, 0:brows] = accum[pl.ds(picked[d], 1), :]

    neighbours = jnp.where(has_up, 1, 0) + jnp.where(has_down, 1, 0)
    pl.semaphore_wait(barrier, n - 1 + neighbours)

    def exchange(kind, src, dst, peer):
        return pltpu.make_async_remote_copy(
            src_ref=src, dst_ref=dst,
            send_sem=send_sem.at[kind, peer], recv_sem=recv_sem.at[kind, me],
            device_id={"table": peer}, device_id_type=MESH,
        )

    def arrival(kind, dst, peer):
        return pltpu.make_async_remote_copy(
            src_ref=dst, dst_ref=dst,
            send_sem=send_sem.at[kind, peer], recv_sem=recv_sem.at[kind, peer],
            device_id={"table": peer}, device_id_type=MESH,
        )

    peers = [lax.rem(me + d, n) for d in range(1, n)]
    for peer in peers:
        exchange(0, ids_send.at[peer], ids.at[rep, me], peer).start()
        exchange(1, grad_send.at[peer], grads.at[rep, me], peer).start()
    for peer in peers:
        exchange(2, mig_send.at[peer], comb.at[blocks + me], peer).start()
    ids[rep, me] = ids_send[me]
    grads[rep, me] = grad_send[me]

    comb[0:blocks, 0:brows, :] = table[...]
    comb[0:blocks, brows:, :] = jnp.zeros((blocks, 8, dim), jnp.float32)
    comb[blocks + me] = jnp.zeros((brows + 8, dim), jnp.float32)
    for j in range(blocks):
        comb[j, brows : brows + 1, 0:brows] = accum[j : j + 1, :]

    for peer in peers:
        arrival(0, ids.at[rep, peer], peer).wait_recv()
        arrival(1, grads.at[rep, peer], peer).wait_recv()

    def hop(kind, way, origin):
        buffer = ids if kind == 0 else grads
        return pltpu.make_async_remote_copy(
            src_ref=buffer.at[origin], dst_ref=buffer.at[origin],
            send_sem=zsend_sem.at[way, kind, origin], recv_sem=zrecv_sem.at[kind, origin],
            device_id={"batch": rep + 1 - 2 * way}, device_id_type=MESH,
        )

    def send_on(way, origin):
        for kind in range(2):
            hop(kind, way, origin).start()

    @pl.when(has_up)
    def _():
        send_on(0, rep)

    @pl.when(has_down)
    def _():
        send_on(1, rep)

    for peer in peers:
        arrival(2, comb.at[blocks + peer], peer).wait_recv()

    row_id = lax.broadcasted_iota(jnp.int32, (brows, 128), 0)

    def counts_of(origin):
        places, counts = [], []
        for g in range(groups):
            named = ids[origin, g * per_group]
            for s in range(1, per_group):
                named = named + ids[origin, g * per_group + s]
            named = named.astype(jnp.int32) - 1
            places.append(jnp.right_shift(named[0:1, :], (brows - 1).bit_length()))
            rows = jnp.bitwise_and(named, brows - 1)
            count = jnp.zeros((brows, 128), jnp.float32)
            for k in range(rows.shape[0]):
                count = count + (rows[k : k + 1, :] == row_id).astype(jnp.float32)
            counts.append(count)
        return jnp.concatenate(places, axis=1), jnp.concatenate(counts, axis=1)

    def chosen(places, counts, first):
        return jnp.concatenate(
            [
                jnp.where(places == first + b, counts, 0.0).astype(jnp.bfloat16)
                for b in range(step_blocks)
            ],
            axis=0,
        )

    span = step_blocks * brows

    def copy_moved(j, carry):
        moved_hl[pl.ds(pl.multiple_of(j * brows, brows), brows), :] = split_halves(
            comb[source[j], 0:brows, :]
        )
        return carry

    lax.fori_loop(0, blocks, copy_moved, 0)

    pool_part[...] = jnp.zeros_like(pool_part)
    places, counts = counts_of(rep)
    gradients = split_halves(grads[rep].reshape(slots, dim))

    def own_step(i, carry):
        hits = chosen(places, counts, i * step_blocks)
        where = pl.ds(pl.multiple_of(i * span, span), span)
        total[where, :] = jnp.dot(hits, gradients, preferred_element_type=jnp.float32)
        both = lax.dot_general(
            hits, moved_hl[where, :], (((0,), (0,)), ((), ())),
            preferred_element_type=jnp.float32,
        )
        pool_part[...] += (both[:, :dim] + both[:, dim:]).reshape(n, cap, dim)
        return carry

    lax.fori_loop(0, blocks // step_blocks, own_step, 0)

    def give_back(peer):
        return pltpu.make_async_remote_copy(
            src_ref=pool_part.at[peer], dst_ref=pool_back.at[me],
            send_sem=psend_sem.at[peer], recv_sem=precv_sem.at[me],
            device_id={"table": peer}, device_id_type=MESH,
        )

    def given_back(peer):
        return pltpu.make_async_remote_copy(
            src_ref=pool_part.at[peer], dst_ref=pool_back.at[peer],
            send_sem=psend_sem.at[peer], recv_sem=precv_sem.at[peer],
            device_id={"table": peer}, device_id_type=MESH,
        )

    for peer in peers:
        give_back(peer).start()
    pool_back[me] = pool_part[me]

    def add_origin(origin):
        places, counts = counts_of(origin)
        gradients = split_halves(grads[origin].reshape(slots, dim))

        def step(i, carry):
            hits = chosen(places, counts, i * step_blocks)
            where = pl.ds(pl.multiple_of(i * span, span), span)
            total[where, :] += jnp.dot(hits, gradients, preferred_element_type=jnp.float32)
            return carry

        lax.fori_loop(0, blocks // step_blocks, step, 0)

    def far_step(h, carry):
        below = rep - h
        above = rep + h

        @pl.when(below >= 0)
        def _():
            for kind in range(2):
                hop(kind, 0, below).wait_recv()

            @pl.when(has_up)
            def _():
                send_on(0, below)

        @pl.when(above < reps)
        def _():
            for kind in range(2):
                hop(kind, 1, above).wait_recv()

            @pl.when(has_down)
            def _():
                send_on(1, above)

        @pl.when(below >= 0)
        def _():
            add_origin(below)

        @pl.when(above < reps)
        def _():
            add_origin(above)

        return carry

    lax.fori_loop(1, reps, far_step, 0)

    eye = lax.broadcasted_iota(jnp.int32, (brows, brows), 0) == lax.broadcasted_iota(
        jnp.int32, (brows, brows), 1
    )

    def update(j, carry):
        where = pl.ds(pl.multiple_of(j * brows, brows), brows)
        both = total[where, :]
        row_grad = both[:, :dim] + both[:, dim:]
        at = source[j]
        old = comb[at, brows : brows + 1, 0:brows]
        old = jnp.sum(jnp.where(eye, old, 0.0), axis=1, keepdims=True)
        new = old + jnp.mean(row_grad * row_grad, axis=1, keepdims=True)
        table_out[j] = comb[at, 0:brows, :] - (LEARN_RATE * row_grad) / (jnp.sqrt(new) + EPSILON)
        accum_out[pl.ds(j, 1), :] = jnp.sum(jnp.where(eye, new, 0.0), axis=0, keepdims=True)
        return carry

    lax.fori_loop(0, blocks, update, 0)

    for peer in peers:
        given_back(peer).wait_recv()
    back = (
        lax.broadcasted_iota(jnp.int32, (samples, slots), 1) == bucket_col[...]
    ).astype(jnp.float32)
    pooled_out[...] = jnp.dot(
        back, pool_back[...].reshape(slots, dim), precision=EXACT,
        preferred_element_type=jnp.float32,
    )

    for peer in peers:
        exchange(0, ids_send.at[peer], ids.at[rep, me], peer).wait_send()
        exchange(1, grad_send.at[peer], grads.at[rep, me], peer).wait_send()
        exchange(2, mig_send.at[peer], comb.at[blocks + me], peer).wait_send()
        give_back(peer).wait_send()

    def drain(origin, carry):
        @pl.when(jnp.logical_and(has_up, origin <= rep))
        def _():
            for kind in range(2):
                hop(kind, 0, origin).wait_send()

        @pl.when(jnp.logical_and(has_down, origin >= rep))
        def _():
            for kind in range(2):
                hop(kind, 1, origin).wait_send()

        return carry

    lax.fori_loop(0, reps, drain, 0)


def gather_kernel(
    n, reps, cap,
    dest, slot, bag_block, bag_rows, accum, table, grad,
    pooled_out, table_out, accum_out,
    comb, mig_send, ids_send, units, ids, moved_hl, total, pool_part, pool_back,
    send_sem, recv_sem, zsend_sem, zrecv_sem, usend_sem, urecv_sem, psend_sem, precv_sem, load_sem, held,
):
    me = lax.axis_index("table")
    rep = lax.axis_index("batch")
    blocks, brows, dim = table.shape
    samples = grad.shape[0]
    slots = n * cap
    groups = slots // 128
    per_group = 128 // cap
    has_up = rep < reps - 1
    has_down = rep > 0
    step_blocks = 4 if blocks % 4 == 0 else 1
    span = step_blocks * brows

    barrier = pltpu.get_barrier_semaphore()
    for d in range(1, n):
        pl.semaphore_signal(
            barrier, inc=1, device_id={"table": lax.rem(me + d, n)}, device_id_type=MESH
        )

    @pl.when(has_up)
    def _():
        pl.semaphore_signal(barrier, inc=1, device_id={"batch": rep + 1}, device_id_type=MESH)

    @pl.when(has_down)
    def _():
        pl.semaphore_signal(barrier, inc=1, device_id={"batch": rep - 1}, device_id_type=MESH)

    load_grad = pltpu.make_async_copy(
        grad, units.at[rep, me, pl.ds(0, samples)], load_sem.at[0]
    )
    load_table = pltpu.make_async_copy(
        table, comb.at[pl.ds(0, blocks), pl.ds(0, brows)], load_sem.at[1]
    )
    load_held = pltpu.make_async_copy(table, held, load_sem.at[2])
    load_grad.start()
    load_held.start()
    load_table.start()

    f32 = jnp.float32
    unit_eye = lax.broadcasted_iota(jnp.int32, (samples, samples), 0) == lax.broadcasted_iota(
        jnp.int32, (samples, samples), 1
    )
    rows_t = lax.dot_general(
        bag_rows[...].astype(f32), unit_eye.astype(f32), (((0,), (0,)), ((), ())),
        precision=EXACT, preferred_element_type=f32,
    )
    named_t = (bag_block[...] * brows).astype(f32) + rows_t
    units[rep, me, samples:, :] = named_t
    load_grad.wait()

    neighbours = jnp.where(has_up, 1, 0) + jnp.where(has_down, 1, 0)
    pl.semaphore_wait(barrier, n - 1 + neighbours)

    def exchange(kind, src, dst, peer):
        return pltpu.make_async_remote_copy(
            src_ref=src, dst_ref=dst,
            send_sem=send_sem.at[kind, peer], recv_sem=recv_sem.at[kind, me],
            device_id={"table": peer}, device_id_type=MESH,
        )

    def arrival(kind, dst, peer):
        return pltpu.make_async_remote_copy(
            src_ref=dst, dst_ref=dst,
            send_sem=send_sem.at[kind, peer], recv_sem=recv_sem.at[kind, peer],
            device_id={"table": peer}, device_id_type=MESH,
        )

    peers = [lax.rem(me + d, n) for d in range(1, n)]

    parity = me % 2
    across = me + 4 - 8 * ((me // 4) % 2)
    along = me + 2 - 4 * ((me // 2) % 2)
    first = across + parity * (along - across)
    second = along + parity * (across - along)
    beside = me + 1 - 2 * parity
    corner = first + second - me

    def hop(way, origin):
        return pltpu.make_async_remote_copy(
            src_ref=units.at[origin, me], dst_ref=units.at[origin, me],
            send_sem=zsend_sem.at[way, origin], recv_sem=zrecv_sem.at[origin],
            device_id={"batch": rep + 1 - 2 * way}, device_id_type=MESH,
        )

    def relay(stage, origin, unit):
        return pltpu.make_async_remote_copy(
            src_ref=units.at[origin, unit], dst_ref=units.at[origin, unit],
            send_sem=usend_sem.at[stage, origin, unit], recv_sem=urecv_sem.at[origin, unit],
            device_id={"table": (first, second, beside)[stage]}, device_id_type=MESH,
        )

    def over(step, body):
        if step == 0:
            body(rep, None)
            return

        @pl.when(rep - step >= 0)
        def _():
            body(rep - step, 0)

        @pl.when(rep + step < reps)
        def _():
            body(rep + step, 1)

    def enter(origin, way):
        if way is not None:
            hop(way, origin).wait_recv()
        if way != 1:
            @pl.when(has_up)
            def _():
                hop(0, origin).start()
        if way != 0:
            @pl.when(has_down)
            def _():
                hop(1, origin).start()
        for stage in range(3):
            relay(stage, origin, me).start()

    def from_first(origin, way):
        relay(0, origin, first).wait_recv()
        relay(1, origin, first).start()
        relay(2, origin, first).start()

    def from_second(origin, way):
        for unit in (second, corner):
            relay(1, origin, unit).wait_recv()
            relay(2, origin, unit).start()

    row_id = lax.broadcasted_iota(jnp.int32, (brows, 128), 0)

    def count_rows(named):
        rows = jnp.bitwise_and(named, brows - 1)
        count = jnp.zeros((brows, 128), jnp.float32)
        for k in range(rows.shape[0]):
            count = count + (rows[k : k + 1, :] == row_id).astype(jnp.float32)
        return jnp.right_shift(named[0:1, :], (brows - 1).bit_length()), count

    def chosen(places, counts, start):
        return jnp.concatenate(
            [
                jnp.where(places == former(start + b), counts, 0.0).astype(jnp.bfloat16)
                for b in range(step_blocks)
            ],
            axis=0,
        )

    def joined(pairs):
        return (
            jnp.concatenate([p for p, _ in pairs], axis=1),
            jnp.concatenate([c for _, c in pairs], axis=1),
        )

    def add_units(origin, which):
        places, counts = joined(
            [
                count_rows(units[origin, u, samples:, :].astype(jnp.int32))
                for u in which
            ]
        )
        gradients = jnp.concatenate(
            [split_halves(units[origin, u, 0:samples, :]) for u in which], axis=0
        )

        def step(i, carry):
            hits = chosen(places, counts, i * step_blocks)
            where = pl.ds(pl.multiple_of(i * span, span), span)
            total[where, :] += jnp.dot(hits, gradients, preferred_element_type=jnp.float32)
            return carry

        lax.fori_loop(0, blocks // step_blocks, step, 0)

    beyond = [u + 1 - 2 * parity for u in (me, first, second, corner)]

    def finish(origin, way):
        for unit in beyond:
            relay(2, origin, unit).wait_recv()
        add_units(origin, [me, first, second, corner] + beyond)

    over(0, enter)

    moving = dest.shape[1]
    count = jnp.int32(0)
    giver = [jnp.int32(0)] * moving
    given = [jnp.int32(0)] * moving
    for s in range(n):
        for k in range(moving):
            hit = dest[s, k] == me
            for r in range(moving):
                now = jnp.logical_and(hit, count == r)
                giver[r] = jnp.where(now, s, giver[r])
                given[r] = jnp.where(now, s * blocks + slot[s, k], given[r])
            count = count + jnp.where(hit, 1, 0)
    freed = [slot[me, r] for r in range(moving)]
    towards = [dest[me, r] for r in range(moving)]

    def source(j):
        at = j
        for r in range(moving):
            at = jnp.where(j == freed[r], blocks + giver[r], at)
        return at

    def former(j):
        at = me * blocks + j
        for r in range(moving):
            at = jnp.where(j == freed[r], given[r], at)
        return at

    owner = jnp.zeros((1, samples), jnp.int32)
    for t in range(1, n):
        owner = owner + (bag_block[...] >= t * blocks).astype(jnp.int32)
    for s in range(n):
        for k in range(moving):
            owner = jnp.where(bag_block[...] == s * blocks + slot[s, k], dest[s, k], owner)
    owner = owner.astype(f32)
    owner_col = jnp.sum(jnp.where(unit_eye, owner, 0.0), axis=1, keepdims=True)
    before = lax.broadcasted_iota(jnp.int32, (samples, samples), 1) < lax.broadcasted_iota(
        jnp.int32, (samples, samples), 0
    )
    within = jnp.sum(
        jnp.where(jnp.logical_and(owner_col == owner, before), 1.0, 0.0), axis=1, keepdims=True
    ).astype(jnp.int32)
    owner_col = owner_col.astype(jnp.int32)
    bucket_col = owner_col * cap + within
    lane_col = owner_col * 128 + (me % per_group) * cap + within
    lanes = (
        lax.broadcasted_iota(jnp.int32, (samples, n * 128), 1) == lane_col
    ).astype(f32)
    sent_ids = jnp.dot(named_t + 1.0, lanes, precision=EXACT, preferred_element_type=f32)
    for d in range(n):
        ids_send[d] = sent_ids[:, d * 128 : (d + 1) * 128]
    for peer in peers:
        exchange(0, ids_send.at[peer], ids.at[me], peer).start()
    load_held.wait()
    load_table.wait()
    for d in range(n):
        picked = jnp.int32(0)
        for r in range(moving):
            picked = jnp.where(towards[r] == d, freed[r], picked)
        mig_send[d, 0:brows, :] = held[picked]
        mig_send[d, brows:, :] = jnp.zeros((8, dim), f32)
        mig_send[d, brows : brows + 1, 0:brows] = accum[pl.ds(picked, 1), :]
    for peer in peers:
        exchange(1, mig_send.at[peer], comb.at[blocks + me], peer).start()
    ids[me] = ids_send[me]
    comb[0:blocks, brows:, :] = jnp.zeros((blocks, 8, dim), jnp.float32)
    comb[blocks + me] = jnp.zeros((brows + 8, dim), jnp.float32)
    for j in range(blocks):
        comb[j, brows : brows + 1, 0:brows] = accum[j : j + 1, :]
    total[...] = jnp.zeros_like(total)
    pool_part[...] = jnp.zeros_like(pool_part)

    if reps > 1:
        over(1, enter)
    over(0, from_first)

    for peer in peers:
        arrival(0, ids.at[peer], peer).wait_recv()
    for peer in peers:
        arrival(1, comb.at[blocks + peer], peer).wait_recv()
    pairs = []
    for g in range(groups):
        named = ids[g * per_group]
        for s in range(1, per_group):
            named = named + ids[g * per_group + s]
        pairs.append(count_rows(named.astype(jnp.int32) - 1))
    asked, asked_counts = joined(pairs)

    def copy_moved(j, carry):
        moved_hl[pl.ds(pl.multiple_of(j * brows, brows), brows), :] = split_halves(
            comb[source(j), 0:brows, :]
        )
        return carry

    lax.fori_loop(0, blocks, copy_moved, 0)

    def pool_step(i, carry):
        where = pl.ds(pl.multiple_of(i * span, span), span)
        both = lax.dot_general(
            chosen(asked, asked_counts, i * step_blocks), moved_hl[where, :],
            (((0,), (0,)), ((), ())), preferred_element_type=jnp.float32,
        )
        pool_part[...] += (both[:, :dim] + both[:, dim:]).reshape(n, cap, dim)
        return carry

    lax.fori_loop(0, blocks // step_blocks, pool_step, 0)

    def give_back(peer, owner):
        return pltpu.make_async_remote_copy(
            src_ref=pool_part.at[peer], dst_ref=pool_back.at[owner],
            send_sem=psend_sem.at[peer], recv_sem=precv_sem.at[owner],
            device_id={"table": peer}, device_id_type=MESH,
        )

    for peer in peers:
        give_back(peer, me).start()
    pool_back[me] = pool_part[me]

    for step in range(2, reps + 4):
        for lag, body in ((0, enter), (1, from_first), (2, from_second)):
            if 0 <= step - lag < reps:
                over(step - lag, body)
        for lag, body in ((3, finish),):
            if 0 <= step - lag < reps:
                over(step - lag, body)

    eye = lax.broadcasted_iota(jnp.int32, (brows, brows), 0) == lax.broadcasted_iota(
        jnp.int32, (brows, brows), 1
    )

    def update(j, carry):
        where = pl.ds(pl.multiple_of(j * brows, brows), brows)
        both = total[where, :]
        row_grad = both[:, :dim] + both[:, dim:]
        at = source(j)
        old = comb[at, brows : brows + 1, 0:brows]
        old = jnp.sum(jnp.where(eye, old, 0.0), axis=1, keepdims=True)
        new = old + jnp.mean(row_grad * row_grad, axis=1, keepdims=True)
        table_out[j] = comb[at, 0:brows, :] - (LEARN_RATE * row_grad) / (jnp.sqrt(new) + EPSILON)
        accum_out[pl.ds(j, 1), :] = jnp.sum(jnp.where(eye, new, 0.0), axis=0, keepdims=True)
        return carry

    lax.fori_loop(0, blocks, update, 0)

    for peer in peers:
        give_back(peer, peer).wait_recv()
    back = (
        lax.broadcasted_iota(jnp.int32, (samples, slots), 1) == bucket_col
    ).astype(jnp.float32)
    pooled_out[...] = jnp.dot(
        back, pool_back[...].reshape(slots, dim), precision=EXACT,
        preferred_element_type=jnp.float32,
    )

    for peer in peers:
        exchange(0, ids_send.at[peer], ids.at[me], peer).wait_send()
        exchange(1, mig_send.at[peer], comb.at[blocks + me], peer).wait_send()
        give_back(peer, me).wait_send()

    def drain(origin, carry):
        @pl.when(jnp.logical_and(has_up, origin <= rep))
        def _():
            hop(0, origin).wait_send()

        @pl.when(jnp.logical_and(has_down, origin >= rep))
        def _():
            hop(1, origin).wait_send()

        for stage, sent in ((0, (me,)), (1, (me, first)), (2, (me, first, second, corner))):
            for unit in sent:
                relay(stage, origin, unit).wait_send()
        return carry

    lax.fori_loop(0, reps, drain, 0)


def per_device(table_rows, accum, plan_dest, plan_slot, bag_block, bag_rows, grad_pooled):
    blocks, brows, dim = table_rows.shape
    n = lax.axis_size("table")
    reps = lax.axis_size("batch")
    me = lax.axis_index("table")
    moving = plan_dest.shape[1]
    samples, pool = bag_rows.shape
    cap = 4 * samples // n
    vmem = pl.BlockSpec(memory_space=pltpu.VMEM)
    smem = pl.BlockSpec(memory_space=pltpu.SMEM)
    slots = n * cap
    f32 = jnp.float32
    out_shape = (
        jax.ShapeDtypeStruct((samples, dim), f32),
        jax.ShapeDtypeStruct((blocks, brows, dim), f32),
        jax.ShapeDtypeStruct((blocks, brows), f32),
    )
    unit_bytes = 4 * (samples + pool) * dim
    if n == 8 and pool == 8 and samples == 128 and n * reps * unit_bytes <= 16 * 1024 * 1024:
        return pl.pallas_call(
            functools.partial(gather_kernel, n, reps, cap),
            out_shape=out_shape,
            in_specs=[smem] * 2 + [vmem] * 3 + [pl.BlockSpec(memory_space=pl.ANY)] * 2,
            out_specs=(vmem, vmem, vmem),
            scratch_shapes=[
                pltpu.VMEM((blocks + n, brows + 8, dim), f32),
                pltpu.VMEM((n, brows + 8, dim), f32),
                pltpu.VMEM((n, pool, 128), f32),
                pltpu.VMEM((reps, n, samples + pool, dim), f32),
                pltpu.VMEM((n, pool, 128), f32),
                pltpu.VMEM((blocks * brows, 2 * dim), jnp.bfloat16),
                pltpu.VMEM((blocks * brows, 2 * dim), f32),
                pltpu.VMEM((n, cap, dim), f32),
                pltpu.VMEM((n, cap, dim), f32),
                pltpu.SemaphoreType.DMA((2, n)),
                pltpu.SemaphoreType.DMA((2, n)),
                pltpu.SemaphoreType.DMA((2, reps)),
                pltpu.SemaphoreType.DMA((reps,)),
                pltpu.SemaphoreType.DMA((3, reps, n)),
                pltpu.SemaphoreType.DMA((reps, n)),
                pltpu.SemaphoreType.DMA((n,)),
                pltpu.SemaphoreType.DMA((n,)),
                pltpu.SemaphoreType.DMA((3,)),
                pltpu.VMEM((blocks, brows, dim), f32),
            ],
            compiler_params=pltpu.CompilerParams(
                collective_id=1, has_side_effects=True, vmem_limit_bytes=48 * 1024 * 1024
            ),
        )(
            plan_dest, plan_slot, bag_block[None, :], bag_rows, accum, table_rows, grad_pooled,
        )

    owners = jnp.arange(n, dtype=jnp.int32)

    targets = plan_dest.reshape(-1)
    sources = jnp.arange(n * moving, dtype=jnp.int32) // moving
    earlier = (targets[:, None] == targets[None, :]) & (sources[None, :] < sources[:, None])
    rank = jnp.sum(earlier.astype(jnp.int32), axis=1)
    landing_at = targets * moving + rank
    every = jnp.arange(n * moving, dtype=jnp.int32)
    landing = jnp.sum(
        jnp.where(landing_at[:, None] == every[None, :], plan_slot.reshape(-1)[None, :], 0), axis=1
    )
    old_spot = sources * blocks + plan_slot.reshape(-1)
    new_spot = targets * blocks + landing

    mine = sources == me
    picked = jnp.sum(
        jnp.where(
            mine[None, :] & (targets[None, :] == owners[:, None]), plan_slot.reshape(-1)[None, :], 0
        ),
        axis=1,
    )
    spots = me * blocks + jnp.arange(blocks, dtype=jnp.int32)
    comes = new_spot[None, :] == spots[:, None]
    source = jnp.where(
        jnp.any(comes, axis=1),
        blocks + jnp.sum(jnp.where(comes, sources[None, :], 0), axis=1),
        jnp.arange(blocks, dtype=jnp.int32),
    )

    moves = bag_block[:, None] == old_spot[None, :]
    read = bag_block + jnp.sum(jnp.where(moves, (new_spot - old_spot)[None, :], 0), axis=1)
    owner = read // blocks
    order = jnp.arange(samples, dtype=jnp.int32)
    slot = jnp.sum(
        ((owner[:, None] == owner[None, :]) & (order[None, :] < order[:, None])).astype(jnp.int32),
        axis=1,
    )
    bucket = owner * cap + slot
    lane = owner * 128 + (me % (128 // cap)) * cap + slot
    rows_t = (((read - owner * blocks) * brows)[None, :] + bag_rows.T + 1).astype(jnp.float32)

    return pl.pallas_call(
        functools.partial(bucket_kernel, n, reps, cap),
        out_shape=out_shape,
        in_specs=[smem] * 2 + [vmem] * 7,
        out_specs=(vmem, vmem, vmem),
        scratch_shapes=[
            pltpu.VMEM((blocks + n, brows + 8, dim), f32),
            pltpu.VMEM((n, brows + 8, dim), f32),
            pltpu.VMEM((n, pool, 128), f32),
            pltpu.VMEM((n, cap, dim), f32),
            pltpu.VMEM((reps, n, cap, dim), f32),
            pltpu.VMEM((reps, n, pool, 128), f32),
            pltpu.VMEM((blocks * brows, 2 * dim), jnp.bfloat16),
            pltpu.VMEM((blocks * brows, 2 * dim), f32),
            pltpu.VMEM((n, cap, dim), f32),
            pltpu.VMEM((n, cap, dim), f32),
            pltpu.SemaphoreType.DMA((3, n)),
            pltpu.SemaphoreType.DMA((3, n)),
            pltpu.SemaphoreType.DMA((2, 2, reps)),
            pltpu.SemaphoreType.DMA((2, reps)),
            pltpu.SemaphoreType.DMA((n,)),
            pltpu.SemaphoreType.DMA((n,)),
        ],
        compiler_params=pltpu.CompilerParams(
            collective_id=0, has_side_effects=True, vmem_limit_bytes=48 * 1024 * 1024
        ),
    )(
        picked, source, bucket[None, :], bucket[:, None], lane[:, None], rows_t,
        table_rows, accum, grad_pooled,
    )


def solution(mesh):
    return jax.shard_map(
        per_device,
        mesh=mesh,
        in_specs=(
            P("table", None, None),
            P("table", None),
            P(),
            P(),
            P(("table", "batch")),
            P(("table", "batch"), None),
            P(("table", "batch"), None),
        ),
        out_specs=(P(("table", "batch"), None), P("table", None, None), P("table", None)),
        check_vma=False,
    )
```
